128 devices in a mesh: fsdp: 16 (over z, y_lo, core), tp: 8 (over y_hi, x).
Axes of the slice: x: 4, y: 4 (y_hi: 2, y_lo: 2; y = y_hi * 2 + y_lo), z: 4, core: 2. Of those that a mesh axis runs over, the one named last changes fastest.
Arguments:
- inputs: bfloat16 [65536, 5120], P(('fsdp', 'tp')), may hold values from -6 to 6
- upstream: bfloat16 [65536, 1024], P(('fsdp', 'tp')), may hold values from -6 to 6
- master: float32 [5120, 1024], P('fsdp'), may hold values from -0.078125 to 0.078125
- moment_one: float32 [5120, 1024], P('fsdp'), may hold values from -3 to 3
- moment_two: float32 [5120, 1024], P('fsdp'), may hold values from 0.1 to 2
- hidden_steps: bfloat16 [4, 64, 5120], P(None, 'fsdp'), may hold values from -6 to 6
- key_weight: bfloat16 [5120, 1024], P(None, 'tp'), may hold values from -0.078125 to 0.078125
- queries: bfloat16 [4, 64, 5120], P(None, 'fsdp', 'tp'), may hold values from -18 to 18
- key_cache: bfloat16 [64, 4096, 1024], P('fsdp', None, 'tp'), may hold values from -18 to 18
- value_cache: bfloat16 [64, 4096, 1024], P('fsdp', None, 'tp'), may hold values from -6 to 6
- lengths: int32 [64], P('fsdp'), may hold values from 512 to 4096, as said below
Outputs:
- input_grad: bfloat16 [65536, 5120], P(('fsdp', 'tp'))
- new_master: float32 [5120, 1024], P('fsdp')
- new_moment: float32 [5120, 1024], P('fsdp')
- fresh_kv: bfloat16 [4, 64, 2, 1024], P(None, 'fsdp', None, 'tp')
- attended: bfloat16 [4, 64, 5120], P(None, 'fsdp', 'tp')
The draws below stay inside these ranges and needn't reach their ends.
Inputs may be any that keep to these rules, and one draw needn't show every extreme that they name: `lengths`: at least one row has a full cache of 4096 slots.
All inputs are finite; a program needn't handle non-finite values.
Results may differ from the reference program's by a relative error of at most 0.0049.
Values may be sent and summed in bfloat16 or wider, within the bound.
A program may use at most 128 MiB of HBM per device.

```python
import math
import jax
import jax.numpy as jnp
from jax import lax

D = 5120
HQ = 40
KV = 8
HD = 128
GROUP = 5
KVD = 1024
TOKENS = 65536
ROWS = 64
CACHE = 4096
STEPS = 4


def draw_queries(key, part):
    key = jax.random.fold_in(key, 1)
    base = jnp.clip(jax.random.normal(key, (STEPS, ROWS, HQ * HD), jnp.float32), -4.0, 4.0)
    return base.astype(jnp.bfloat16)


def draw_key_cache(key, part):
    key = jax.random.fold_in(key, 2)
    base = jnp.clip(jax.random.normal(key, (ROWS, CACHE, KV * HD), jnp.float32), -4.0, 4.0)
    return base.astype(jnp.bfloat16)


def draw_lengths(key, part):
    key = jax.random.fold_in(key, 3)
    drawn = jax.random.randint(key, (ROWS,), CACHE // 8, CACHE + 1)
    chosen = jax.random.randint(jax.random.fold_in(key, 4), (), 0, ROWS)
    return jnp.where(jnp.arange(ROWS) == chosen, CACHE, drawn).astype(jnp.int32)


def block_levels(stream_key, dims, cuts, smallest, top_value):
    factor_of, own = 1.0, jax.random.fold_in(stream_key, 6)
    for position, blocks in cuts:
        heights = jnp.exp(jax.random.uniform(jax.random.fold_in(own, position), (blocks,), jnp.float32, smallest / len(cuts), top_value / len(cuts)))
        factor_of = factor_of * jnp.repeat(heights, dims[position] // blocks).reshape([-1 if axis == position else 1 for axis in range(len(dims))])
    return factor_of


def scatter_about(own_key, extent, width, bound, cuts=(), dtype=jnp.bfloat16):
    values = jax.random.normal(own_key, extent, jnp.float32) * width
    if len(cuts) > 0:
        values = block_levels(own_key, extent, cuts, -0.22, 0.18) * values
    return jnp.clip(values, min=-bound, max=bound).astype(dtype)


def setup_inputs(seed: int = 0) -> dict:
    splits = jax.random.split(jax.random.key(seed), 12)
    return {
        "inputs": scatter_about(splits[0], (TOKENS, D), 1.0, 6.0, ((0, 128),)),
        "upstream": scatter_about(splits[1], (TOKENS, KVD), 1.0, 6.0, ((0, 128),)),
        "master": scatter_about(splits[2], (D, KVD), D ** -0.5, 0.078125, ((0, 16),), jnp.float32),
        "moment_one": scatter_about(splits[3], (D, KVD), 0.5, 3.0, ((0, 16),), jnp.float32),
        "moment_two": jnp.clip(jnp.exp(math.log(2.0) - 2.9957323 * jax.random.uniform(splits[4], (D, KVD), jnp.float32) ** block_levels(splits[4], (D, KVD), ((0, 16),), -0.2, 0.2)), 0.1, 2.0),
        "hidden_steps": scatter_about(splits[5], (STEPS, ROWS, D), 1.0, 6.0, ((1, 16),)),
        "key_weight": scatter_about(splits[6], (D, KVD), D ** -0.5, 0.078125, ((1, 8),)),
        "queries": draw_queries(jax.random.fold_in(splits[11], 71), 0),
        "key_cache": draw_key_cache(jax.random.fold_in(splits[11], 71), 0),
        "value_cache": scatter_about(splits[9], (ROWS, CACHE, KVD), 1.0, 6.0, ((0, 16), (2, 8))),
        "lengths": draw_lengths(jax.random.fold_in(splits[11], 71), 0),
    }


beta_one = 0.9
beta_two = 0.95
learn_rate = 0.004
decay_rate = 0.1
adam_eps = 1e-08
correction_one = 1.0 - 0.9 ** 20
correction_two = 1.0 - 0.95 ** 20

def adamw(master, grad, moment_one, moment_two):
    new_first = beta_one * moment_one + (1.0 - beta_one) * grad
    new_second = beta_two * moment_two + (1.0 - beta_two) * grad * grad
    update = new_first / correction_one / (jnp.sqrt(new_second / correction_two) + adam_eps)
    return (master - learn_rate * (update + decay_rate * master), new_first)

def attend_row(items):
    query_heads, cache_keys, cache_values, fresh_keys, fresh_values, length = items
    scale = 1.0 / math.sqrt(HD)
    query_heads = query_heads.astype(jnp.float32).reshape(STEPS, KV, GROUP, HD)
    cache_keys = cache_keys.astype(jnp.float32).reshape(CACHE, KV, HD)
    cache_values = cache_values.astype(jnp.float32).reshape(CACHE, KV, HD)
    fresh_keys = fresh_keys.astype(jnp.float32).reshape(STEPS, KV, HD)
    fresh_values = fresh_values.astype(jnp.float32).reshape(STEPS, KV, HD)
    cache_scores = jnp.einsum('skgd,ckd->skgc', query_heads, cache_keys) * scale
    fresh_scores = jnp.einsum('skgd,tkd->skgt', query_heads, fresh_keys) * scale
    slots = lax.broadcasted_iota(jnp.int32, (1, 1, 1, CACHE), 3)
    cache_scores = jnp.where(slots < length, cache_scores, -1e+30)
    later = lax.broadcasted_iota(jnp.int32, (STEPS, 1, 1, STEPS), 3)
    now = lax.broadcasted_iota(jnp.int32, (STEPS, 1, 1, STEPS), 0)
    fresh_scores = jnp.where(later <= now, fresh_scores, -1e+30)
    highest = jnp.maximum(lax.optimization_barrier(jnp.max(cache_scores, axis=-1)), lax.optimization_barrier(jnp.max(fresh_scores, axis=-1)))[..., None]
    cache_exp = jnp.exp(cache_scores - highest)
    fresh_exp = jnp.exp(fresh_scores - highest)
    normalizer = lax.optimization_barrier(jnp.sum(cache_exp, axis=-1, keepdims=True)) + lax.optimization_barrier(jnp.sum(fresh_exp, axis=-1, keepdims=True))
    cache_prob = (cache_exp / normalizer).astype(jnp.bfloat16).astype(jnp.float32)
    fresh_prob = (fresh_exp / normalizer).astype(jnp.bfloat16).astype(jnp.float32)
    result = jnp.einsum('skgc,ckd->skgd', cache_prob, cache_values) + jnp.einsum('skgt,tkd->skgd', fresh_prob, fresh_values)
    return result.reshape(STEPS, HQ * HD).astype(jnp.bfloat16)

def reference(inputs, upstream, master, moment_one, moment_two, hidden_steps, key_weight, queries, key_cache, value_cache, lengths):
    weight = master.astype(jnp.bfloat16)
    input_grad = jnp.dot(upstream, weight.T, preferred_element_type=jnp.float32).astype(jnp.bfloat16)
    grad = lax.dot_general(inputs, upstream, (((0,), (0,)), ((), ())), preferred_element_type=jnp.float32)
    grad = grad * (1.0 / math.sqrt(TOKENS))
    new_master, new_moment = adamw(master, grad, moment_one, moment_two)
    new_weight = new_master.astype(jnp.bfloat16)
    flat = hidden_steps.reshape(STEPS * ROWS, D)
    fresh_keys = jnp.dot(flat, key_weight, preferred_element_type=jnp.float32).astype(jnp.bfloat16).reshape(STEPS, ROWS, KVD)
    fresh_values = jnp.dot(flat, new_weight, preferred_element_type=jnp.float32).astype(jnp.bfloat16).reshape(STEPS, ROWS, KVD)
    fresh_kv = jnp.stack([fresh_keys, fresh_values], axis=2)
    per_row = lax.map(attend_row, (jnp.transpose(queries, (1, 0, 2)), key_cache, value_cache, jnp.transpose(fresh_keys, (1, 0, 2)), jnp.transpose(fresh_values, (1, 0, 2)), lengths.astype(jnp.int32)))
    attended = jnp.transpose(per_row, (1, 0, 2))
    return (input_grad, new_master, new_moment, fresh_kv, attended)
```

```python
import functools
import math

import jax
import jax.numpy as jnp
from jax import lax
from jax.experimental import pallas as pl
from jax.experimental.pallas import tpu as pltpu
from jax.sharding import PartitionSpec as P

HD = 128
GROUP = 5
MESH = pl.DeviceIdType.MESH


beta_one = 0.9
beta_two = 0.95
learn_rate = 0.004
decay_rate = 0.1
adam_eps = 1e-08
correction_one = 1.0 - 0.9**20
correction_two = 1.0 - 0.95**20

A1, B1, C1, A2, B2, C2, A3, B3, C3 = 0, 12, 24, 27, 39, 42, 45, 48, 51
XS, UT, GX, TP, HS, FR, SEMS = 54, 58, 59, 60, 68, 84, 100

f32, bf16 = jnp.float32, jnp.bfloat16


def adamw(master, grad, moment_one, moment_two):
    new_first = beta_one * moment_one + (1.0 - beta_one) * grad
    new_second = beta_two * moment_two + (1.0 - beta_two) * grad * grad
    update = new_first / correction_one / (jnp.sqrt(new_second / correction_two) + adam_eps)
    return (master - learn_rate * (update + decay_rate * master), new_first)


def learn_kernel(
    grad_factor,
    x_hbm,
    ut,
    master_hbm,
    m1_hbm,
    m2_hbm,
    hidden,
    new_master,
    new_moment,
    fresh_out,
    x_own,
    x_sib,
    ut_sib,
    master,
    m1,
    m2,
    ga,
    gb,
    gc,
    r1a,
    r1b,
    r1c,
    s1a,
    s1b,
    s1c,
    r2a,
    r2b,
    r2c,
    s2a,
    s2b,
    s2c,
    r3a,
    r3b,
    r3c,
    gx,
    gt,
    gall,
    wpad,
    hr,
    pf,
    fr,
    ssem,
    rsem,
    lsem,
):
    f, t = lax.axis_index("fsdp"), lax.axis_index("tp")
    z, yl, c = f // 4, (f // 2) % 2, f % 2
    yh, x = t // 4, t % 4
    y = yh * 2 + yl
    sib = (z * 4 + yl * 2 + (1 - c), t)

    def at_x(d):
        return (x + d) % 4

    def dev_x(d):
        return (f, yh * 4 + (x + d) % 4)

    def dev_y(d):
        yy = (y + d) % 4
        return (z * 4 + (yy % 2) * 2 + c, (yy // 2) * 4 + x)

    def dev_z(d):
        return (((z + d) % 4) * 4 + yl * 2 + c, t)

    def rcopy(src, dst, n, who):
        return pltpu.make_async_remote_copy(
            src_ref=src,
            dst_ref=dst,
            send_sem=ssem.at[n],
            recv_sem=rsem.at[n],
            device_id=who,
            device_id_type=MESH,
        )

    def lanes(zz):
        return pl.ds(pl.multiple_of(zz * 1280, 1280), 1280)

    x_copies = [
        pltpu.make_async_copy(
            x_hbm.at[:, lanes((z + 1 + k) % 4)], x_own.at[:, lanes((z + 1 + k) % 4)], lsem.at[k]
        )
        for k in range(4)
    ]
    opt_copies = [
        pltpu.make_async_copy(a, b, lsem.at[4 + i])
        for i, (a, b) in enumerate([(master_hbm, master), (m1_hbm, m1), (m2_hbm, m2)])
    ]
    for cp in x_copies + opt_copies:
        cp.start()

    barrier = pltpu.get_barrier_semaphore()

    @pl.loop(1, 16)
    def _(j):
        pl.semaphore_signal(barrier, 1, device_id=((f + j) % 16, t), device_id_type=MESH)

    @pl.loop(1, 8)
    def _(j):
        pl.semaphore_signal(barrier, 1, device_id=(f, (t + j) % 8), device_id_type=MESH)

    pl.semaphore_signal(
        barrier,
        1,
        device_id=(z * 4 + (1 - yl) * 2 + c, (1 - yh) * 4 + x),
        device_id_type=MESH,
    )
    pl.semaphore_wait(barrier, 23)

    ut_copy = rcopy(ut.at[1 - c], ut_sib, UT, sib)
    ut_copy.start()
    sib_copies = [
        rcopy(x_hbm.at[:, lanes((z + 1 + k) % 4)], x_sib.at[:, lanes((z + 1 + k) % 4)], XS + k, sib)
        for k in range(4)
    ]
    for cp in sib_copies:
        cp.start()

    def hidden_copy(j):
        to = (f + j) % 16
        cols = pl.ds(pl.multiple_of((to // 2) * 640, 640), 640)
        return rcopy(hidden.at[:, cols], hr.at[j], HS + j, (to, t))

    @pl.loop(1, 16)
    def _(j):
        hidden_copy(j).start()

    hr[0] = hidden[:, pl.ds(pl.multiple_of((f // 2) * 640, 640), 640)]
    wpad[...] = jnp.zeros_like(wpad)

    def a1(d, zz, k):
        return rcopy(
            ga.at[at_x(d), :, zz], r1a.at[d - 1, :, zz], A1 + (d - 1) * 4 + k, dev_x(d)
        )

    def b1(d, zz, k):
        yy = (y + d) % 4
        return rcopy(
            gb.at[:, yy // 2, zz, yy % 2], r1b.at[d - 1, :, zz], B1 + (d - 1) * 4 + k, dev_y(d)
        )

    def c1(d):
        return rcopy(gc.at[:, :, (z + d) % 4], r1c.at[d - 1], C1 + d - 1, dev_z(d))

    def a2(d, zz, k):
        yy = (y + d) % 4
        return rcopy(
            s1a.at[yy // 2, zz, yy % 2], r2a.at[d - 1, zz], A2 + (d - 1) * 4 + k, dev_y(d)
        )

    def b2(d):
        return rcopy(s1b.at[:, (z + d) % 4], r2b.at[d - 1], B2 + d - 1, dev_z(d))

    def c2(d):
        return rcopy(s1c.at[at_x(d)], r2c.at[d - 1], C2 + d - 1, dev_x(d))

    def a3(d):
        return rcopy(s2a.at[(z + d) % 4], r3a.at[d - 1], A3 + d - 1, dev_z(d))

    def b3(d):
        return rcopy(s2b.at[at_x(d)], r3b.at[d - 1], B3 + d - 1, dev_x(d))

    def c3(d):
        yy = (y + d) % 4
        return rcopy(s2c.at[yy // 2, yy % 2], r3c.at[d - 1], C3 + d - 1, dev_y(d))

    ut_copy.wait()
    for k in range(4):
        zz = (z + 1 + k) % 4
        x_copies[k].wait()
        sib_copies[k].wait()

        @pl.loop(0, 4)
        def _(i):
            ll, half = i // 2, i % 2
            cols = pl.ds(pl.multiple_of(zz * 1280 + ll * 640, 640), 640)
            rows = pl.ds(pl.multiple_of(half * 256, 256), 256)
            part = jnp.dot(ut[c, rows], x_own[:, cols], preferred_element_type=f32)
            part += jnp.dot(ut_sib[rows], x_sib[:, cols], preferred_element_type=f32)
            part = part.astype(bf16)
            for b in range(4):
                xx, hh = half * 2 + b // 2, b % 2
                ga[xx, hh, zz, ll] = part[b * 64 : (b + 1) * 64, 0:256]
                gb[xx, hh, zz, ll] = part[b * 64 : (b + 1) * 64, 256:512]
                gc[xx, hh, zz, ll] = part[b * 64 : (b + 1) * 64, 512:640]

        for d in (2, 1, 3):
            a1(d, zz, k).start()
            b1(d, zz, k).start()
        if k < 3:
            c1(k + 1).start()

    def total(own, others, index):
        got = own.astype(f32)
        for d in range(3):
            got += others[(d,) + index].astype(f32)
        return got

    for k in range(4):
        zz = (z + 1 + k) % 4
        for d in (1, 2, 3):
            a1(d, zz, k).wait()

        @pl.loop(0, 4)
        def _(i):
            hh, ll = i // 2, i % 2
            s1a[hh, zz, ll] = total(ga[x, hh, zz, ll], r1a, (hh, zz, ll)).astype(bf16)

        for d in (2, 1, 3):
            a2(d, zz, k).start()
        for d in (1, 2, 3):
            b1(d, zz, k).wait()

        @pl.loop(0, 4)
        def _(i):
            s1b[i, zz] = total(gb[i, yh, zz, yl], r1b, (i, zz)).astype(bf16)

        if k < 3:
            b2(k + 1).start()
    for d in (1, 2, 3):
        c1(d).wait()

    @pl.loop(0, 16)
    def _(i):
        xx, hh, ll = i // 4, (i // 2) % 2, i % 2
        s1c[xx, hh, ll] = total(gc[xx, hh, z, ll], r1c, (xx, hh, ll)).astype(bf16)

    for d in (2, 1, 3):
        c2(d).start()

    for k in range(4):
        zz = (z + 1 + k) % 4
        for d in (1, 2, 3):
            a2(d, zz, k).wait()
        s2a[zz] = total(s1a[yh, zz, yl], r2a, (zz,))
        if k < 3:
            a3(k + 1).start()
    for d in (1, 2, 3):
        b2(d).wait()

    @pl.loop(0, 4)
    def _(i):
        s2b[i] = total(s1b[i, z], r2b, (i,))

    for d in (2, 1, 3):
        b3(d).start()
    for d in (1, 2, 3):
        c2(d).wait()

    @pl.loop(0, 4)
    def _(i):
        hh, ll = i // 2, i % 2
        s2c[hh, ll] = total(s1c[x, hh, ll], r2c, (hh, ll))

    for d in (2, 1, 3):
        c3(d).start()

    for d in (1, 2, 3):
        a3(d).wait()
        b3(d).wait()
        c3(d).wait()
    gx[c, :, 0:256] = total(s2a[z], r3a, ()) * grad_factor
    gx[c, :, 256:512] = total(s2b[x], r3b, ()) * grad_factor
    gx[c, :, 512:640] = total(s2c[yh, yl], r3c, ()) * grad_factor
    gx_copy = rcopy(gx.at[c], gx.at[c], GX, sib)
    gx_copy.start()
    gx_copy.wait()
    gt[...] = gx[...].reshape(128, 640).T
    mine = pl.ds(pl.multiple_of(c * 320, 320), 320)
    gall[t] = gt[mine, :].astype(bf16)

    def tp_copy(j):
        return rcopy(gall.at[t], gall.at[t], TP + j, (f, (t + j) % 8))

    @pl.loop(1, 8)
    def _(j):
        tp_copy(j).start()

    for cp in opt_copies:
        cp.wait()

    def update(tt):
        cols = pl.ds(pl.multiple_of(tt * 128, 128), 128)
        nm, nf = adamw(master[:, cols], gall[tt].astype(f32), m1[:, cols], m2[:, cols])
        new_master[:, cols] = nm
        new_moment[:, cols] = nf
        return nm

    wpad[mine, :] = update(t).astype(bf16)

    @pl.loop(1, 16)
    def _(j):
        hidden_copy(j).wait()

    pf[...] = jnp.dot(
        hr[...].reshape(256, 640), wpad[...], preferred_element_type=f32
    ).reshape(16, 16, 128)

    def fresh_copy(j):
        return rcopy(pf.at[j], fr.at[j], FR + j, ((f + 16 - j) % 16, t))

    @pl.loop(1, 16)
    def _(j):
        fresh_copy(j).start()

    @pl.loop(1, 8)
    def _(j):
        tp_copy(j).wait()
        update((t + 8 - j) % 8)

    @pl.loop(1, 16)
    def _(j):
        fresh_copy(j).wait()

    fr[0] = pf[0]
    fresh_out[...] = jnp.sum(fr[...], axis=0)


def learn(inputs, upstream, master, m1, m2, flat, grad_factor):
    tokens, width = inputs.shape
    ut = upstream.reshape(tokens, 2, 4, 2, 64).transpose(3, 2, 1, 4, 0).reshape(2, 512, tokens)
    hbm = pl.BlockSpec(memory_space=pl.ANY)
    vmem = pl.BlockSpec(memory_space=pltpu.VMEM)
    shape = jax.ShapeDtypeStruct
    V = pltpu.VMEM
    scratch = [
        V((512, 5120), bf16),
        V((512, 5120), bf16),
        V((512, 512), bf16),
        V((320, 1024), f32),
        V((320, 1024), f32),
        V((320, 1024), f32),
        V((4, 2, 4, 2, 64, 256), bf16),
        V((4, 2, 4, 2, 64, 256), bf16),
        V((4, 2, 4, 2, 64, 128), bf16),
        V((3, 2, 4, 2, 64, 256), bf16),
        V((3, 4, 4, 64, 256), bf16),
        V((3, 4, 2, 2, 64, 128), bf16),
        V((2, 4, 2, 64, 256), bf16),
        V((4, 4, 64, 256), bf16),
        V((4, 2, 2, 64, 128), bf16),
        V((3, 4, 64, 256), bf16),
        V((3, 4, 64, 256), bf16),
        V((3, 2, 2, 64, 128), bf16),
        V((4, 64, 256), f32),
        V((4, 64, 256), f32),
        V((2, 2, 64, 128), f32),
        V((3, 64, 256), f32),
        V((3, 64, 256), f32),
        V((3, 64, 128), f32),
        V((2, 64, 640), f32),
        V((640, 128), f32),
        V((8, 320, 128), bf16),
        V((640, 128), bf16),
        V((16, 16, 640), bf16),
        V((16, 16, 128), f32),
        V((16, 16, 128), f32),
        pltpu.SemaphoreType.DMA((SEMS,)),
        pltpu.SemaphoreType.DMA((SEMS,)),
        pltpu.SemaphoreType.DMA((7,)),
    ]
    return pl.pallas_call(
        functools.partial(learn_kernel, grad_factor),
        out_shape=(
            shape((320, 1024), f32),
            shape((320, 1024), f32),
            shape((16, 128), f32),
        ),
        in_specs=[hbm, vmem, hbm, hbm, hbm, vmem],
        out_specs=[vmem, vmem, vmem],
        scratch_shapes=scratch,
        name="learn",
        cost_estimate=pl.CostEstimate(
            flops=60_000_000_000, bytes_accessed=160_000_000, transcendentals=0
        ),
        compiler_params=pltpu.CompilerParams(
            collective_id=0, has_side_effects=True, vmem_limit_bytes=56 << 20
        ),
    )(inputs, ut, master, m1, m2, flat)


def shards(
    inputs,
    upstream,
    master,
    moment_one,
    moment_two,
    hidden_steps,
    key_weight,
    queries,
    key_cache,
    value_cache,
    lengths,
):
    weight = master.astype(jnp.bfloat16)
    grad_factor = 1.0 / math.sqrt(inputs.shape[0] * lax.axis_size("fsdp") * lax.axis_size("tp"))
    steps_count, rows_here, model_width = hidden_steps.shape
    flat = hidden_steps.reshape(steps_count * rows_here, model_width)
    gathered = lax.all_gather(weight, "fsdp", axis=0, tiled=True)
    new_master, new_moment, value_proj = learn(
        inputs, upstream, master, moment_one, moment_two, flat, grad_factor
    )
    product = lax.dot_general(
        upstream,
        gathered,
        (((1,), (1,)), ((), ())),
        preferred_element_type=jnp.float32,
    )
    input_grad = product.astype(jnp.bfloat16)
    local_cols = key_weight.shape[1]
    fresh_keys = (
        jnp.dot(flat, key_weight, preferred_element_type=jnp.float32)
        .astype(jnp.bfloat16)
        .reshape(steps_count, rows_here, local_cols)
    )
    fresh_values = value_proj.astype(jnp.bfloat16).reshape(steps_count, rows_here, local_cols)
    fresh_kv = jnp.stack([fresh_keys, fresh_values], axis=2)
    heads_here = local_cols // HD
    cache_len = key_cache.shape[1]
    scale = 1.0 / math.sqrt(HD)
    query_heads = queries.reshape(steps_count, rows_here, heads_here, GROUP, HD)
    cache_keys = key_cache.reshape(rows_here, cache_len, heads_here, HD)
    cache_values = value_cache.reshape(rows_here, cache_len, heads_here, HD)
    new_keys = fresh_keys.reshape(steps_count, rows_here, heads_here, HD)
    new_values = fresh_values.reshape(steps_count, rows_here, heads_here, HD)
    cache_scores = (
        jnp.einsum("srkgd,rckd->srkgc", query_heads, cache_keys, preferred_element_type=jnp.float32)
        * scale
    )
    fresh_scores = (
        jnp.einsum("srkgd,trkd->srkgt", query_heads, new_keys, preferred_element_type=jnp.float32)
        * scale
    )
    slots = lax.broadcasted_iota(jnp.int32, (1, rows_here, 1, 1, cache_len), 4)
    cache_scores = jnp.where(slots < lengths.reshape(1, rows_here, 1, 1, 1), cache_scores, -1e30)
    later = lax.broadcasted_iota(jnp.int32, (steps_count, 1, 1, 1, steps_count), 4)
    now = lax.broadcasted_iota(jnp.int32, (steps_count, 1, 1, 1, steps_count), 0)
    fresh_scores = jnp.where(later <= now, fresh_scores, -1e30)
    highest = jnp.maximum(jnp.max(cache_scores, axis=-1), jnp.max(fresh_scores, axis=-1))[..., None]
    cache_exp = jnp.exp(cache_scores - highest)
    fresh_exp = jnp.exp(fresh_scores - highest)
    normalizer = jnp.sum(cache_exp, axis=-1, keepdims=True) + jnp.sum(
        fresh_exp, axis=-1, keepdims=True
    )
    cache_prob = (cache_exp / normalizer).astype(jnp.bfloat16)
    fresh_prob = (fresh_exp / normalizer).astype(jnp.bfloat16)
    result = jnp.einsum(
        "srkgc,rckd->srkgd", cache_prob, cache_values, preferred_element_type=jnp.float32
    )
    result = result + jnp.einsum(
        "srkgt,trkd->srkgd", fresh_prob, new_values, preferred_element_type=jnp.float32
    )
    attended = result.reshape(steps_count, rows_here, heads_here * GROUP * HD).astype(jnp.bfloat16)
    return (input_grad, new_master, new_moment, fresh_kv, attended)


def solution(mesh):
    in_specs = (
        P(("fsdp", "tp"), None),
        P(("fsdp", "tp"), None),
        P("fsdp", None),
        P("fsdp", None),
        P("fsdp", None),
        P(None, "fsdp", None),
        P(None, "tp"),
        P(None, "fsdp", "tp"),
        P("fsdp", None, "tp"),
        P("fsdp", None, "tp"),
        P("fsdp"),
    )
    out_specs = (
        P(("fsdp", "tp"), None),
        P("fsdp", None),
        P("fsdp", None),
        P(None, "fsdp", None, "tp"),
        P(None, "fsdp", "tp"),
    )
    return jax.shard_map(shards, mesh=mesh, in_specs=in_specs, out_specs=out_specs, check_vma=False)
```

```python
import functools
import math

import jax
import jax.numpy as jnp
from jax import lax
from jax.experimental import pallas as pl
from jax.experimental.pallas import tpu as pltpu
from jax.sharding import PartitionSpec as P

HD = 128
GROUP = 5
MESH = pl.DeviceIdType.MESH


beta_one = 0.9
beta_two = 0.95
learn_rate = 0.004
decay_rate = 0.1
adam_eps = 1e-08
correction_one = 1.0 - 0.9**20
correction_two = 1.0 - 0.95**20

A1, B1, C1, A2, B2, C2, A3, B3, C3 = 0, 12, 24, 27, 39, 42, 45, 48, 51
XS, UT, GX, TP, HS, FR = 54, 58, 59, 60, 68, 84
WZ, WY, WX, WS, SEMS = 100, 106, 122, 143, 151
WHOLE, QUARTER = 192, 32

f32, bf16 = jnp.float32, jnp.bfloat16


def adamw(master, grad, moment_one, moment_two):
    new_first = beta_one * moment_one + (1.0 - beta_one) * grad
    new_second = beta_two * moment_two + (1.0 - beta_two) * grad * grad
    update = new_first / correction_one / (jnp.sqrt(new_second / correction_two) + adam_eps)
    return (master - learn_rate * (update + decay_rate * master), new_first)


def learn_kernel(
    grad_factor,
    x_hbm,
    u,
    master_hbm,
    m1_hbm,
    m2_hbm,
    hidden,
    kw_hbm,
    queries,
    k_hbm,
    v_hbm,
    lengths,
    grad_hbm,
    new_master,
    new_moment,
    fresh_out,
    attended,
    ut,
    wall,
    kw,
    keys,
    values,
    qf,
    acc,
    fprob,
    x_own,
    x_sib,
    ut_sib,
    master,
    m1,
    m2,
    ga,
    gb,
    gc,
    r1a,
    r1b,
    r1c,
    s1a,
    s1b,
    s1c,
    r2a,
    r2b,
    r2c,
    s2a,
    s2b,
    s2c,
    r3a,
    r3b,
    r3c,
    gx,
    gt,
    gall,
    wpad,
    hr,
    pf,
    fr,
    ssem,
    rsem,
    lsem,
):
    f, t = lax.axis_index("fsdp"), lax.axis_index("tp")
    z, yl, c = f // 4, (f // 2) % 2, f % 2
    yh, x = t // 4, t % 4
    y = yh * 2 + yl
    sib = (z * 4 + yl * 2 + (1 - c), t)

    def at_x(d):
        return (x + d) % 4

    def dev_x(d):
        return (f, yh * 4 + (x + d) % 4)

    def dev_y(d):
        yy = (y + d) % 4
        return (z * 4 + (yy % 2) * 2 + c, (yy // 2) * 4 + x)

    def dev_z(d):
        return (((z + d) % 4) * 4 + yl * 2 + c, t)

    def rcopy(src, dst, n, who):
        return pltpu.make_async_remote_copy(
            src_ref=src,
            dst_ref=dst,
            send_sem=ssem.at[n],
            recv_sem=rsem.at[n],
            device_id=who,
            device_id_type=MESH,
        )

    def lanes(zz):
        return pl.ds(pl.multiple_of(zz * 1280, 1280), 1280)

    x_copies = [
        pltpu.make_async_copy(
            x_hbm.at[:, lanes((z + 1 + k) % 4)], x_own.at[:, lanes((z + 1 + k) % 4)], lsem.at[k]
        )
        for k in range(4)
    ]
    opt_copies = [
        pltpu.make_async_copy(a, b, lsem.at[4 + i])
        for i, (a, b) in enumerate([(master_hbm, master), (m1_hbm, m1), (m2_hbm, m2)])
    ]
    attn_copies = [
        pltpu.make_async_copy(a, b, lsem.at[7 + i])
        for i, (a, b) in enumerate([(kw_hbm, kw), (k_hbm, keys), (v_hbm, values)])
    ]
    for cp in opt_copies[:1] + x_copies + attn_copies + opt_copies[1:]:
        cp.start()

    barrier = pltpu.get_barrier_semaphore()

    @pl.loop(1, 16)
    def _(j):
        pl.semaphore_signal(barrier, 1, device_id=((f + j) % 16, t), device_id_type=MESH)

    @pl.loop(1, 8)
    def _(j):
        pl.semaphore_signal(barrier, 1, device_id=(f, (t + j) % 8), device_id_type=MESH)

    pl.semaphore_signal(
        barrier,
        1,
        device_id=(z * 4 + (1 - yl) * 2 + c, (1 - yh) * 4 + x),
        device_id_type=MESH,
    )
    own = z * 2 + yl
    opt_copies[0].wait()
    wall[own, c] = master[...].astype(bf16)
    for tt in range(8):
        block = u[:, tt * 128 : (tt + 1) * 128].T
        place = ((tt % 4) * 2 + tt // 4) * 64
        ut[0, place : place + 64] = block[0:64]
        ut[1, place : place + 64] = block[64:128]
    pl.semaphore_wait(barrier, 23)

    ut_copy = rcopy(ut.at[1 - c], ut_sib, UT, sib)
    ut_copy.start()
    sib_copies = [
        rcopy(x_hbm.at[:, lanes((z + 1 + k) % 4)], x_sib.at[:, lanes((z + 1 + k) % 4)], XS + k, sib)
        for k in range(4)
    ]
    for cp in sib_copies:
        cp.start()

    quarter = WHOLE + x * QUARTER

    def wz(d, part):
        rows = (pl.ds(0, WHOLE), pl.ds(pl.multiple_of(quarter, 32), QUARTER))[part]
        piece = wall.at[own, c, rows]
        return rcopy(piece, piece, WZ + (d - 1) * 2 + part, dev_z(d))

    def wy(dz, way, part):
        first = (way * (WHOLE // 2), pl.multiple_of(quarter + way * (QUARTER // 2), 16))[part]
        rows = pl.ds(first, (WHOLE // 2, QUARTER // 2)[part])
        piece = wall.at[((z + dz) % 4) * 2 + yl, c, rows]
        return rcopy(piece, piece, WY + (dz * 2 + way) * 2 + part, dev_y(1 if way == 0 else 3))

    def wx(dz, other, d):
        ll = 1 - yl if other else yl
        rows = pl.ds(pl.multiple_of(quarter, 32), QUARTER)
        piece = wall.at[((z + dz) % 4) * 2 + ll, c, rows]
        return rcopy(piece, piece, WX + (other * 3 + dz + other - 1) * 3 + d - 1, dev_x(d))

    def ws(dz, other):
        ll = 1 - yl if other else yl
        piece = wall.at[((z + dz) % 4) * 2 + ll, c]
        return rcopy(piece, piece, WS + other * 4 + dz, sib)

    def grad_out(dz, other):
        ll = 1 - yl if other else yl
        cols = pl.ds(pl.multiple_of((((z + dz) % 4) * 2 + ll) * 640, 640), 640)
        return pltpu.make_async_copy(
            x_own.at[:, cols], grad_hbm.at[:, cols], lsem.at[10 + other * 4 + dz]
        )

    def input_grads(other):
        @pl.loop(0, 4)
        def _(dz):
            ll = 1 - yl if other else yl
            ss = ((z + dz) % 4) * 2 + ll
            cols = pl.ds(pl.multiple_of(ss * 640, 640), 640)
            x_own[:, cols] = lax.dot_general(
                u[...],
                wall[ss].reshape(640, 1024),
                (((1,), (1,)), ((), ())),
                preferred_element_type=f32,
            ).astype(bf16)
            grad_out(dz, other).start()

    for d in (2, 1, 3):
        for part in range(2):
            wz(d, part).start()
    for way in range(2):
        for part in range(2):
            wy(0, way, part).start()

    def hidden_copy(j):
        to = (f + j) % 16
        cols = pl.ds(pl.multiple_of((to // 2) * 640, 640), 640)
        return rcopy(hidden.at[:, cols], hr.at[j], HS + j, (to, t))

    @pl.loop(1, 16)
    def _(j):
        hidden_copy(j).start()

    hr[0] = hidden[:, pl.ds(pl.multiple_of((f // 2) * 640, 640), 640)]
    wpad[...] = jnp.zeros_like(wpad)

    def a1(d, zz, k):
        return rcopy(
            ga.at[at_x(d), :, zz], r1a.at[d - 1, :, zz], A1 + (d - 1) * 4 + k, dev_x(d)
        )

    def b1(d, zz, k):
        yy = (y + d) % 4
        return rcopy(
            gb.at[:, yy // 2, zz, yy % 2], r1b.at[d - 1, :, zz], B1 + (d - 1) * 4 + k, dev_y(d)
        )

    def c1(d):
        return rcopy(gc.at[:, :, (z + d) % 4], r1c.at[d - 1], C1 + d - 1, dev_z(d))

    def a2(d, zz, k):
        yy = (y + d) % 4
        return rcopy(
            s1a.at[yy // 2, zz, yy % 2], r2a.at[d - 1, zz], A2 + (d - 1) * 4 + k, dev_y(d)
        )

    def b2(d):
        return rcopy(s1b.at[:, (z + d) % 4], r2b.at[d - 1], B2 + d - 1, dev_z(d))

    def c2(d):
        return rcopy(s1c.at[at_x(d)], r2c.at[d - 1], C2 + d - 1, dev_x(d))

    def a3(d):
        return rcopy(s2a.at[(z + d) % 4], r3a.at[d - 1], A3 + d - 1, dev_z(d))

    def b3(d):
        return rcopy(s2b.at[at_x(d)], r3b.at[d - 1], B3 + d - 1, dev_x(d))

    def c3(d):
        yy = (y + d) % 4
        return rcopy(s2c.at[yy // 2, yy % 2], r3c.at[d - 1], C3 + d - 1, dev_y(d))

    ut_copy.wait()
    for k in range(4):
        zz = (z + 1 + k) % 4
        x_copies[k].wait()
        sib_copies[k].wait()

        @pl.loop(0, 4)
        def _(i):
            ll, half = i // 2, i % 2
            cols = pl.ds(pl.multiple_of(zz * 1280 + ll * 640, 640), 640)
            rows = pl.ds(pl.multiple_of(half * 256, 256), 256)
            part = jnp.dot(ut[c, rows], x_own[:, cols], preferred_element_type=f32)
            part += jnp.dot(ut_sib[rows], x_sib[:, cols], preferred_element_type=f32)
            part = part.astype(bf16)
            for b in range(4):
                xx, hh = half * 2 + b // 2, b % 2
                ga[xx, hh, zz, ll] = part[b * 64 : (b + 1) * 64, 0:256]
                gb[xx, hh, zz, ll] = part[b * 64 : (b + 1) * 64, 256:512]
                gc[xx, hh, zz, ll] = part[b * 64 : (b + 1) * 64, 512:640]

        for d in (2, 1, 3):
            a1(d, zz, k).start()
            b1(d, zz, k).start()
        if k < 3:
            c1(k + 1).start()

    ws(0, 0).start()

    attn_copies[0].wait()
    fresh_keys = jnp.dot(hidden[...], kw[...], preferred_element_type=f32).astype(bf16)
    fresh_out[0] = fresh_keys
    qf[...] = jnp.zeros_like(qf)
    for step in range(4):
        for g in range(GROUP):
            qf[:, step * GROUP + g] = queries[step, :, g * HD : (g + 1) * HD].astype(f32)
    attn_copies[1].wait()
    attn_copies[2].wait()
    scale = 1.0 / math.sqrt(HD)
    nt = (((1,), (1,)), ((), ()))

    @pl.loop(0, 4)
    def _(r):
        q = qf[r].astype(bf16)
        scores = lax.dot_general(q, keys[r], nt, preferred_element_type=f32) * scale
        slots = lax.broadcasted_iota(jnp.int32, (32, 4096), 1)
        scores = jnp.where(slots < lengths[r], scores, -1e30)
        extra = lax.dot_general(q, fresh_out[0], nt, preferred_element_type=f32) * scale
        line = lax.broadcasted_iota(jnp.int32, (32, 16), 0)
        item = lax.broadcasted_iota(jnp.int32, (32, 16), 1)
        seen = ((item & 3) == r) & ((item >> 2) * GROUP <= line)
        extra = jnp.where(seen, extra, -1e30)
        highest = jnp.maximum(
            jnp.max(scores, axis=1, keepdims=True), jnp.max(extra, axis=1, keepdims=True)
        )
        scores = jnp.exp(scores - highest)
        extra = jnp.exp(extra - highest)
        norm = 1.0 / (
            jnp.sum(scores, axis=1, keepdims=True) + jnp.sum(extra, axis=1, keepdims=True)
        )
        fprob[r] = (extra * norm).astype(bf16)
        acc[r] = jnp.dot((scores * norm).astype(bf16), values[r], preferred_element_type=f32)

    for d in (1, 3, 2):
        for part in range(2):
            wz(d, part).wait()
    for dz in (1, 2, 3):
        for way in range(2):
            for part in range(2):
                wy(dz, way, part).start()
        for d in (2, 1, 3):
            wx(dz, 0, d).start()

    def total(own, others, index):
        got = own.astype(f32)
        for d in range(3):
            got += others[(d,) + index].astype(f32)
        return got

    for k in range(4):
        zz = (z + 1 + k) % 4
        for d in (1, 2, 3):
            a1(d, zz, k).wait()

        @pl.loop(0, 4)
        def _(i):
            hh, ll = i // 2, i % 2
            s1a[hh, zz, ll] = total(ga[x, hh, zz, ll], r1a, (hh, zz, ll)).astype(bf16)

        for d in (2, 1, 3):
            a2(d, zz, k).start()
        for d in (1, 2, 3):
            b1(d, zz, k).wait()

        @pl.loop(0, 4)
        def _(i):
            s1b[i, zz] = total(gb[i, yh, zz, yl], r1b, (i, zz)).astype(bf16)

        if k < 3:
            b2(k + 1).start()
    for d in (1, 2, 3):
        c1(d).wait()

    @pl.loop(0, 16)
    def _(i):
        xx, hh, ll = i // 4, (i // 2) % 2, i % 2
        s1c[xx, hh, ll] = total(gc[xx, hh, z, ll], r1c, (xx, hh, ll)).astype(bf16)

    for d in (2, 1, 3):
        c2(d).start()

    for dz in range(4):
        for way in range(2):
            for part in range(2):
                wy(dz, way, part).wait()
        for d in (2, 1, 3):
            wx(dz, 1, d).start()

    for k in range(4):
        zz = (z + 1 + k) % 4
        for d in (1, 2, 3):
            a2(d, zz, k).wait()
        s2a[zz] = total(s1a[yh, zz, yl], r2a, (zz,))
        if k < 3:
            a3(k + 1).start()
    for d in (1, 2, 3):
        b2(d).wait()

    @pl.loop(0, 4)
    def _(i):
        s2b[i] = total(s1b[i, z], r2b, (i,))

    for d in (2, 1, 3):
        b3(d).start()
    for d in (1, 2, 3):
        c2(d).wait()

    @pl.loop(0, 4)
    def _(i):
        hh, ll = i // 2, i % 2
        s2c[hh, ll] = total(s1c[x, hh, ll], r2c, (hh, ll))

    for d in (2, 1, 3):
        c3(d).start()

    for dz in (1, 2, 3):
        for d in (1, 2, 3):
            wx(dz, 0, d).wait()
        ws(dz, 0).start()
    for dz in range(4):
        ws(dz, 0).wait()
    input_grads(0)

    for d in (1, 2, 3):
        a3(d).wait()
        b3(d).wait()
        c3(d).wait()
    gx[c, :, 0:256] = total(s2a[z], r3a, ()) * grad_factor
    gx[c, :, 256:512] = total(s2b[x], r3b, ()) * grad_factor
    gx[c, :, 512:640] = total(s2c[yh, yl], r3c, ()) * grad_factor
    gx_copy = rcopy(gx.at[c], gx.at[c], GX, sib)
    gx_copy.start()
    gx_copy.wait()
    gt[...] = gx[...].reshape(128, 640).T
    mine = pl.ds(pl.multiple_of(c * 320, 320), 320)
    gall[t] = gt[mine, :].astype(bf16)

    def tp_copy(j):
        return rcopy(gall.at[t], gall.at[t], TP + j, (f, (t + j) % 8))

    @pl.loop(1, 8)
    def _(j):
        tp_copy(j).start()

    for cp in opt_copies[1:]:
        cp.wait()

    def update(tt):
        cols = pl.ds(pl.multiple_of(tt * 128, 128), 128)
        nm, nf = adamw(master[:, cols], gall[tt].astype(f32), m1[:, cols], m2[:, cols])
        new_master[:, cols] = nm
        new_moment[:, cols] = nf
        return nm

    wpad[mine, :] = update(t).astype(bf16)

    @pl.loop(1, 16)
    def _(j):
        hidden_copy(j).wait()

    pf[...] = jnp.dot(
        hr[...].reshape(256, 640), wpad[...], preferred_element_type=f32
    ).reshape(16, 16, 128)

    def fresh_copy(j):
        return rcopy(pf.at[j], fr.at[j], FR + j, ((f + 16 - j) % 16, t))

    @pl.loop(1, 16)
    def _(j):
        fresh_copy(j).start()

    for dz in range(4):
        for d in (1, 2, 3):
            wx(dz, 1, d).wait()
        ws(dz, 1).start()

    @pl.loop(1, 8)
    def _(j):
        tp_copy(j).wait()
        update((t + 8 - j) % 8)

    @pl.loop(1, 16)
    def _(j):
        fresh_copy(j).wait()

    fr[0] = pf[0]
    fresh_out[1] = jnp.sum(fr[...], axis=0).astype(bf16)

    @pl.loop(0, 4)
    def _(r):
        acc[r] += jnp.dot(fprob[r], fresh_out[1], preferred_element_type=f32)

    for step in range(4):
        for g in range(GROUP):
            attended[step, :, g * HD : (g + 1) * HD] = acc[:, step * GROUP + g].astype(bf16)

    for dz in range(4):
        ws(dz, 1).wait()
    input_grads(1)
    for other in range(2):
        for dz in range(4):
            grad_out(dz, other).wait()


def learn(
    inputs, upstream, master, m1, m2, flat, key_weight, queries, keys, values, lengths, grad_factor
):
    hbm = pl.BlockSpec(memory_space=pl.ANY)
    vmem = pl.BlockSpec(memory_space=pltpu.VMEM)
    smem = pl.BlockSpec(memory_space=pltpu.SMEM)
    shape = jax.ShapeDtypeStruct
    V = pltpu.VMEM
    scratch = [
        V((2, 512, 512), bf16),
        V((8, 2, 320, 1024), bf16),
        V((5120, 128), bf16),
        V((4, 4096, 128), bf16),
        V((4, 4096, 128), bf16),
        V((4, 32, 128), f32),
        V((4, 32, 128), f32),
        V((4, 32, 16), bf16),
        V((512, 5120), bf16),
        V((512, 5120), bf16),
        V((512, 512), bf16),
        V((320, 1024), f32),
        V((320, 1024), f32),
        V((320, 1024), f32),
        V((4, 2, 4, 2, 64, 256), bf16),
        V((4, 2, 4, 2, 64, 256), bf16),
        V((4, 2, 4, 2, 64, 128), bf16),
        V((3, 2, 4, 2, 64, 256), bf16),
        V((3, 4, 4, 64, 256), bf16),
        V((3, 4, 2, 2, 64, 128), bf16),
        V((2, 4, 2, 64, 256), bf16),
        V((4, 4, 64, 256), bf16),
        V((4, 2, 2, 64, 128), bf16),
        V((3, 4, 64, 256), bf16),
        V((3, 4, 64, 256), bf16),
        V((3, 2, 2, 64, 128), bf16),
        V((4, 64, 256), f32),
        V((4, 64, 256), f32),
        V((2, 2, 64, 128), f32),
        V((3, 64, 256), f32),
        V((3, 64, 256), f32),
        V((3, 64, 128), f32),
        V((2, 64, 640), f32),
        V((640, 128), f32),
        V((8, 320, 128), bf16),
        V((640, 128), bf16),
        V((16, 16, 640), bf16),
        V((16, 16, 128), f32),
        V((16, 16, 128), f32),
        pltpu.SemaphoreType.DMA((SEMS,)),
        pltpu.SemaphoreType.DMA((SEMS,)),
        pltpu.SemaphoreType.DMA((18,)),
    ]
    return pl.pallas_call(
        functools.partial(learn_kernel, grad_factor),
        out_shape=(
            shape((512, 5120), bf16),
            shape((320, 1024), f32),
            shape((320, 1024), f32),
            shape((2, 16, 128), bf16),
            shape((4, 4, 640), bf16),
        ),
        in_specs=[hbm, vmem, hbm, hbm, hbm, vmem, hbm, vmem, hbm, hbm, smem],
        out_specs=[hbm, vmem, vmem, vmem, vmem],
        scratch_shapes=scratch,
        name="learn",
        cost_estimate=pl.CostEstimate(
            flops=60_000_000_000, bytes_accessed=160_000_000, transcendentals=0
        ),
        compiler_params=pltpu.CompilerParams(
            collective_id=0, has_side_effects=True, vmem_limit_bytes=60 << 20
        ),
    )(inputs, upstream, master, m1, m2, flat, key_weight, queries, keys, values, lengths)


def shards(
    inputs,
    upstream,
    master,
    moment_one,
    moment_two,
    hidden_steps,
    key_weight,
    queries,
    key_cache,
    value_cache,
    lengths,
):
    grad_factor = 1.0 / math.sqrt(inputs.shape[0] * lax.axis_size("fsdp") * lax.axis_size("tp"))
    flat = hidden_steps.reshape(16, 5120)
    input_grad, new_master, new_moment, fresh, attended = learn(
        inputs,
        upstream,
        master,
        moment_one,
        moment_two,
        flat,
        key_weight,
        queries,
        key_cache,
        value_cache,
        lengths,
        grad_factor,
    )
    fresh_kv = fresh.reshape(2, 4, 4, 128).transpose(1, 2, 0, 3)
    return (input_grad, new_master, new_moment, fresh_kv, attended)


def solution(mesh):
    in_specs = (
        P(("fsdp", "tp"), None),
        P(("fsdp", "tp"), None),
        P("fsdp", None),
        P("fsdp", None),
        P("fsdp", None),
        P(None, "fsdp", None),
        P(None, "tp"),
        P(None, "fsdp", "tp"),
        P("fsdp", None, "tp"),
        P("fsdp", None, "tp"),
        P("fsdp"),
    )
    out_specs = (
        P(("fsdp", "tp"), None),
        P("fsdp", None),
        P("fsdp", None),
        P(None, "fsdp", None, "tp"),
        P(None, "fsdp", "tp"),
    )
    return jax.shard_map(shards, mesh=mesh, in_specs=in_specs, out_specs=out_specs, check_vma=False)
```

```python
import functools
import math

import jax
import jax.numpy as jnp
from jax import lax
from jax.experimental import pallas as pl
from jax.experimental.pallas import tpu as pltpu
from jax.sharding import PartitionSpec as P

HD = 128
GROUP = 5
MESH = pl.DeviceIdType.MESH


beta_one = 0.9
beta_two = 0.95
learn_rate = 0.004
decay_rate = 0.1
adam_eps = 1e-08
correction_one = 1.0 - 0.9**20
correction_two = 1.0 - 0.95**20

T1, D1, F1, C1, A2, C2, A3, C3 = 0, 8, 16, 24, 27, 39, 42, 45
XS, UT, GX, TP, HS, FR = 48, 52, 53, 54, 62, 78
WZ, WF, WY, WS, SEMS = 94, 96, 98, 106, 114
NT = (((1,), (1,)), ((), ()))

f32, bf16 = jnp.float32, jnp.bfloat16


def adamw(master, grad, moment_one, moment_two):
    new_first = beta_one * moment_one + (1.0 - beta_one) * grad
    new_second = beta_two * moment_two + (1.0 - beta_two) * grad * grad
    update = new_first / correction_one / (jnp.sqrt(new_second / correction_two) + adam_eps)
    return (master - learn_rate * (update + decay_rate * master), new_first)


def learn_kernel(
    grad_factor,
    x_hbm,
    u,
    master_hbm,
    m1_hbm,
    m2_hbm,
    hidden,
    kw_hbm,
    queries,
    k_hbm,
    v_hbm,
    lengths,
    wall,
    gall,
    fresh_out,
    attended,
    ut,
    wown,
    kw,
    keys,
    values,
    qf,
    acc,
    fprob,
    x_own,
    x_sib,
    ut_sib,
    master,
    m1,
    m2,
    ga,
    gc,
    t1,
    r1a,
    r1c,
    s1a,
    s1c,
    r2a,
    r2c,
    s2a,
    s2c,
    r3a,
    r3c,
    gx,
    gt,
    gown,
    wpad,
    hr,
    pf,
    fr,
    ssem,
    rsem,
    lsem,
):
    f, t = lax.axis_index("fsdp"), lax.axis_index("tp")
    z, yl, c = f // 4, (f // 2) % 2, f % 2
    yh, x = t // 4, t % 4
    y = yh * 2 + yl
    sib = (z * 4 + yl * 2 + (1 - c), t)
    own = z * 2 + yl

    def dev_x(d):
        return (f, yh * 4 + (x + d) % 4)

    def dev_y(d):
        yy = (y + d) % 4
        return (z * 4 + (yy % 2) * 2 + c, (yy // 2) * 4 + x)

    def dev_z(d):
        return (((z + d) % 4) * 4 + yl * 2 + c, t)

    def rcopy(src, dst, n, who):
        return pltpu.make_async_remote_copy(
            src_ref=src,
            dst_ref=dst,
            send_sem=ssem.at[n],
            recv_sem=rsem.at[n],
            device_id=who,
            device_id_type=MESH,
        )

    def lanes(zz):
        return pl.ds(pl.multiple_of(zz * 1280, 1280), 1280)

    tcols = pl.ds(pl.multiple_of(t * 128, 128), 128)
    local = [(master_hbm, master)]
    local += [(x_hbm.at[:, lanes((z + k) % 4)], x_own.at[:, lanes((z + k) % 4)]) for k in (1, 2, 3, 4)]
    local += [(kw_hbm, kw), (k_hbm, keys), (v_hbm, values)]
    local += [(m1_hbm.at[:, tcols], m1), (m2_hbm.at[:, tcols], m2)]
    local = [pltpu.make_async_copy(a, b, lsem.at[i]) for i, (a, b) in enumerate(local)]
    for cp in local:
        cp.start()
    own_out = pltpu.make_async_copy(wown, wall.at[own, c], lsem.at[10])
    grad_out = pltpu.make_async_copy(gown, gall.at[t], lsem.at[11])

    barrier = pltpu.get_barrier_semaphore()

    @pl.loop(1, 16)
    def _(j):
        pl.semaphore_signal(barrier, 1, device_id=((f + j) % 16, t), device_id_type=MESH)

    @pl.loop(1, 8)
    def _(j):
        pl.semaphore_signal(barrier, 1, device_id=(f, (t + j) % 8), device_id_type=MESH)

    pl.semaphore_signal(
        barrier,
        1,
        device_id=(z * 4 + (1 - yl) * 2 + c, (1 - yh) * 4 + x),
        device_id_type=MESH,
    )

    for tt in range(8):
        block = u[:, tt * 128 : (tt + 1) * 128].T
        place = ((tt % 4) * 2 + tt // 4) * 64
        ut[0, place : place + 64] = block[0:64]
        ut[1, place : place + 64] = block[64:128]
    local[0].wait()
    wown[...] = master[...].astype(bf16)
    own_out.start()
    pl.semaphore_wait(barrier, 23)

    ut_copy = rcopy(ut.at[1 - c], ut_sib, UT, sib)
    ut_copy.start()
    sib_copies = [
        rcopy(x_hbm.at[:, lanes((z + k) % 4)], x_sib.at[:, lanes((z + k) % 4)], XS + k - 1, sib)
        for k in (1, 2, 3, 4)
    ]
    for cp in sib_copies:
        cp.start()

    def wz(i):
        return rcopy(wown, wall.at[own, c], WZ + i, dev_z(1 if i == 0 else 3))

    def wf(i):
        rows = pl.ds(i * 160, 160)
        piece = wall.at[((z + (3 if i == 0 else 1)) % 4) * 2 + yl, c, rows]
        return rcopy(piece, piece, WF + i, dev_z(1 if i == 0 else 3))

    def wy(dz, way):
        rows = pl.ds(way * 160, 160)
        piece = wall.at[((z + dz) % 4) * 2 + yl, c, rows]
        source = wown.at[rows] if dz == 0 else piece
        return rcopy(source, piece, WY + dz * 2 + way, dev_y(1 if way == 0 else 3))

    def ws(dz, other):
        ll = 1 - yl if other else yl
        piece = wall.at[((z + dz) % 4) * 2 + ll, c]
        source = wown if (dz, other) == (0, 0) else piece
        return rcopy(source, piece, WS + other * 4 + dz, sib)

    for i in range(2):
        wz(i).start()
    for way in range(2):
        wy(0, way).start()

    def hidden_copy(j):
        to = (f + j) % 16
        cols = pl.ds(pl.multiple_of((to // 2) * 640, 640), 640)
        return rcopy(hidden.at[:, cols], hr.at[j], HS + j, (to, t))

    @pl.loop(1, 16)
    def _(j):
        hidden_copy(j).start()

    hr[0] = hidden[:, pl.ds(pl.multiple_of((f // 2) * 640, 640), 640)]
    wpad[...] = jnp.zeros_like(wpad)

    right, left = (x + 1) % 4, (x + 3) % 4

    def two_hop(i, zz, k):
        return rcopy(
            ga.at[(x + 2) % 4, i, zz], t1.at[i, zz], T1 + i * 4 + k, dev_x(1 if i == 0 else 3)
        )

    def direct(i, zz, k):
        piece = ga.at[right if i == 0 else left, 1 - i, zz]
        return rcopy(piece, r1a.at[i, 1 - i, zz], D1 + i * 4 + k, dev_x(1 if i == 0 else 3))

    def summed(i, zz, k):
        piece = ga.at[right if i == 0 else left, i, zz]
        return rcopy(piece, r1a.at[i, i, zz], F1 + i * 4 + k, dev_x(1 if i == 0 else 3))

    def c1(d):
        return rcopy(gc.at[:, :, (z + d) % 4], r1c.at[d - 1], C1 + d - 1, dev_z(d))

    def a2(d, zz, k):
        yy = (y + d) % 4
        return rcopy(
            s1a.at[yy // 2, zz, yy % 2], r2a.at[d - 1, zz], A2 + (d - 1) * 4 + k, dev_y(d)
        )

    def c2(d):
        return rcopy(s1c.at[(x + d) % 4], r2c.at[d - 1], C2 + d - 1, dev_x(d))

    def a3(d):
        return rcopy(s2a.at[(z + d) % 4], r3a.at[d - 1], A3 + d - 1, dev_z(d))

    def c3(d):
        yy = (y + d) % 4
        return rcopy(s2c.at[yy // 2, yy % 2], r3c.at[d - 1], C3 + d - 1, dev_y(d))

    def pass_on(k):
        zz = (z + 1 + k) % 4
        for i in range(2):
            two_hop(i, zz, k).wait()
            to = right if i == 0 else left

            @pl.loop(0, 2)
            def _(ll):
                got = ga[to, i, zz, ll].astype(f32) + t1[i, zz, ll].astype(f32)
                ga[to, i, zz, ll] = got.astype(bf16)

            summed(i, zz, k).start()

    ut_copy.wait()
    for k in range(4):
        zz = (z + 1 + k) % 4
        local[1 + k].wait()
        sib_copies[k].wait()

        @pl.loop(0, 4)
        def _(i):
            ll, half = i // 2, i % 2
            cols = pl.ds(pl.multiple_of(zz * 1280 + ll * 640, 640), 640)
            rows = pl.ds(pl.multiple_of(half * 256, 256), 256)
            part = jnp.dot(ut[c, rows], x_own[:, cols], preferred_element_type=f32)
            part += jnp.dot(ut_sib[rows], x_sib[:, cols], preferred_element_type=f32)
            part = part.astype(bf16)
            for b in range(4):
                xx, hh = half * 2 + b // 2, b % 2
                ga[xx, hh, zz, ll] = part[b * 64 : (b + 1) * 64, 0:512]
                gc[xx, hh, zz, ll] = part[b * 64 : (b + 1) * 64, 512:640]

        for i in range(2):
            two_hop(i, zz, k).start()
        for i in range(2):
            direct(i, zz, k).start()
        if k < 3:
            c1(k + 1).start()
        if k > 0:
            pass_on(k - 1)
    pass_on(3)
    ws(0, 0).start()

    for i in range(2):
        wz(i).wait()
    for i in range(2):
        wf(i).start()
    for dz in (1, 3):
        for way in range(2):
            wy(dz, way).start()
        ws(dz, 0).start()

    local[5].wait()
    fresh_out[0] = jnp.dot(hidden[...], kw[...], preferred_element_type=f32).astype(bf16)
    qf[...] = jnp.zeros_like(qf)
    for step in range(4):
        for g in range(GROUP):
            qf[:, step * GROUP + g] = queries[step, :, g * HD : (g + 1) * HD].astype(f32)
    local[6].wait()
    local[7].wait()
    scale = 1.0 / math.sqrt(HD)

    def attend(r):
        q = qf[r].astype(bf16)
        scores = lax.dot_general(q, keys[r], NT, preferred_element_type=f32) * scale
        slots = lax.broadcasted_iota(jnp.int32, (32, 4096), 1)
        scores = jnp.where(slots < lengths[r], scores, -1e30)
        extra = lax.dot_general(q, fresh_out[0], NT, preferred_element_type=f32) * scale
        line = lax.broadcasted_iota(jnp.int32, (32, 16), 0)
        item = lax.broadcasted_iota(jnp.int32, (32, 16), 1)
        seen = ((item & 3) == r) & ((item >> 2) * GROUP <= line)
        extra = jnp.where(seen, extra, -1e30)
        highest = jnp.maximum(
            jnp.max(scores, axis=1, keepdims=True), jnp.max(extra, axis=1, keepdims=True)
        )
        scores = jnp.exp(scores - highest)
        extra = jnp.exp(extra - highest)
        norm = 1.0 / (
            jnp.sum(scores, axis=1, keepdims=True) + jnp.sum(extra, axis=1, keepdims=True)
        )
        fprob[r] = (extra * norm).astype(bf16)
        acc[r] = jnp.dot((scores * norm).astype(bf16), values[r], preferred_element_type=f32)

    def total(own, others, index, count=3):
        got = own.astype(f32)
        for d in range(count):
            got += others[(d,) + index].astype(f32)
        return got

    for k in range(4):
        zz = (z + 1 + k) % 4
        for i in range(2):
            direct(i, zz, k).wait()
            summed(i, zz, k).wait()

        @pl.loop(0, 4)
        def _(i):
            hh, ll = i // 2, i % 2
            s1a[hh, zz, ll] = total(ga[x, hh, zz, ll], r1a, (hh, zz, ll), 2).astype(bf16)

        for d in (2, 1, 3):
            a2(d, zz, k).start()

        @pl.loop(k, k + 1)
        def _(r):
            attend(r)

    for i in range(2):
        wf(i).wait()
    for way in range(2):
        wy(2, way).start()
    ws(2, 0).start()
    for d in (1, 2, 3):
        c1(d).wait()

    @pl.loop(0, 16)
    def _(i):
        xx, hh, ll = i // 4, (i // 2) % 2, i % 2
        s1c[xx, hh, ll] = total(gc[xx, hh, z, ll], r1c, (xx, hh, ll)).astype(bf16)

    for d in (2, 1, 3):
        c2(d).start()

    for k in range(4):
        zz = (z + 1 + k) % 4
        for d in (1, 2, 3):
            a2(d, zz, k).wait()
        s2a[zz] = total(s1a[yh, zz, yl], r2a, (zz,))
        if k < 3:
            a3(k + 1).start()
    for d in (1, 2, 3):
        c2(d).wait()

    @pl.loop(0, 4)
    def _(i):
        hh, ll = i // 2, i % 2
        s2c[hh, ll] = total(s1c[x, hh, ll], r2c, (hh, ll))

    for d in (2, 1, 3):
        c3(d).start()

    for d in (1, 2, 3):
        a3(d).wait()
        c3(d).wait()
    gx[c, :, 0:512] = total(s2a[z], r3a, ()) * grad_factor
    gx[c, :, 512:640] = total(s2c[yh, yl], r3c, ()) * grad_factor
    gx_copy = rcopy(gx.at[c], gx.at[c], GX, sib)
    gx_copy.start()
    gx_copy.wait()
    gt[...] = gx[...].reshape(128, 640).T
    mine = pl.ds(pl.multiple_of(c * 320, 320), 320)
    gown[...] = gt[mine, :].astype(bf16)
    grad_out.start()

    def tp_copy(j):
        return rcopy(gown, gall.at[t], TP + j, (f, (t + j) % 8))

    @pl.loop(1, 8)
    def _(j):
        tp_copy(j).start()

    local[8].wait()
    local[9].wait()
    stepped, _ = adamw(master[:, tcols], gown[...].astype(f32), m1[...], m2[...])
    wpad[mine, :] = stepped.astype(bf16)

    @pl.loop(1, 16)
    def _(j):
        hidden_copy(j).wait()

    pf[...] = jnp.dot(
        hr[...].reshape(256, 640), wpad[...], preferred_element_type=f32
    ).reshape(16, 16, 128)

    def fresh_copy(j):
        return rcopy(pf.at[j], fr.at[j], FR + j, ((f + 16 - j) % 16, t))

    @pl.loop(1, 16)
    def _(j):
        fresh_copy(j).start()

    for dz in (0, 1, 3, 2):
        for way in range(2):
            wy(dz, way).wait()
        ws(dz, 1).start()

    @pl.loop(1, 16)
    def _(j):
        fresh_copy(j).wait()

    fr[0] = pf[0]
    fresh_out[1] = jnp.sum(fr[...], axis=0).astype(bf16)

    @pl.loop(0, 4)
    def _(r):
        acc[r] += jnp.dot(fprob[r], fresh_out[1], preferred_element_type=f32)

    for step in range(4):
        for g in range(GROUP):
            attended[step, :, g * HD : (g + 1) * HD] = acc[:, step * GROUP + g].astype(bf16)

    own_out.wait()
    grad_out.wait()

    @pl.loop(1, 8)
    def _(j):
        tp_copy(j).wait()

    for other in range(2):
        for dz in range(4):
            ws(dz, other).wait()


def learn(
    inputs, upstream, master, m1, m2, flat, key_weight, queries, keys, values, lengths, grad_factor
):
    hbm = pl.BlockSpec(memory_space=pl.ANY)
    vmem = pl.BlockSpec(memory_space=pltpu.VMEM)
    smem = pl.BlockSpec(memory_space=pltpu.SMEM)
    shape = jax.ShapeDtypeStruct
    V = pltpu.VMEM
    scratch = [
        V((2, 512, 512), bf16),
        V((320, 1024), bf16),
        V((5120, 128), bf16),
        V((4, 4096, 128), bf16),
        V((4, 4096, 128), bf16),
        V((4, 32, 128), f32),
        V((4, 32, 128), f32),
        V((4, 32, 16), bf16),
        V((512, 5120), bf16),
        V((512, 5120), bf16),
        V((512, 512), bf16),
        V((320, 1024), f32),
        V((320, 128), f32),
        V((320, 128), f32),
        V((4, 2, 4, 2, 64, 512), bf16),
        V((4, 2, 4, 2, 64, 128), bf16),
        V((2, 4, 2, 64, 512), bf16),
        V((2, 2, 4, 2, 64, 512), bf16),
        V((3, 4, 2, 2, 64, 128), bf16),
        V((2, 4, 2, 64, 512), bf16),
        V((4, 2, 2, 64, 128), bf16),
        V((3, 4, 64, 512), bf16),
        V((3, 2, 2, 64, 128), bf16),
        V((4, 64, 512), f32),
        V((2, 2, 64, 128), f32),
        V((3, 64, 512), f32),
        V((3, 64, 128), f32),
        V((2, 64, 640), f32),
        V((640, 128), f32),
        V((320, 128), bf16),
        V((640, 128), bf16),
        V((16, 16, 640), bf16),
        V((16, 16, 128), f32),
        V((16, 16, 128), f32),
        pltpu.SemaphoreType.DMA((SEMS,)),
        pltpu.SemaphoreType.DMA((SEMS,)),
        pltpu.SemaphoreType.DMA((12,)),
    ]
    return pl.pallas_call(
        functools.partial(learn_kernel, grad_factor),
        out_shape=(
            shape((8, 2, 320, 1024), bf16),
            shape((8, 320, 128), bf16),
            shape((2, 16, 128), bf16),
            shape((4, 4, 640), bf16),
        ),
        in_specs=[hbm, vmem, hbm, hbm, hbm, vmem, hbm, vmem, hbm, hbm, smem],
        out_specs=[hbm, hbm, vmem, vmem],
        scratch_shapes=scratch,
        name="learn",
        compiler_params=pltpu.CompilerParams(
            collective_id=0, has_side_effects=True, vmem_limit_bytes=56 << 20
        ),
    )(inputs, upstream, master, m1, m2, flat, key_weight, queries, keys, values, lengths)


def finish_kernel(u, w, grad, master, m1, m2, input_grad, new_master, new_moment):
    input_grad[...] = lax.dot_general(u[...], w[...], NT, preferred_element_type=f32).astype(bf16)
    new_master[...], new_moment[...] = adamw(
        master[...], grad[...].astype(f32), m1[...], m2[...]
    )


def finish(upstream, weight, grad, master, m1, m2):
    cols = pl.BlockSpec((320, 128), lambda i: (0, i))
    return pl.pallas_call(
        finish_kernel,
        grid=(8,),
        out_shape=(
            jax.ShapeDtypeStruct((512, 5120), bf16),
            jax.ShapeDtypeStruct((320, 1024), f32),
            jax.ShapeDtypeStruct((320, 1024), f32),
        ),
        in_specs=[
            pl.BlockSpec((512, 1024), lambda i: (0, 0)),
            pl.BlockSpec((640, 1024), lambda i: (i, 0)),
            pl.BlockSpec((None, 320, 128), lambda i: (i, 0, 0)),
            cols,
            cols,
            cols,
        ],
        out_specs=[pl.BlockSpec((512, 640), lambda i: (0, i)), cols, cols],
        name="finish",
        compiler_params=pltpu.CompilerParams(vmem_limit_bytes=32 << 20),
    )(upstream, weight, grad, master, m1, m2)


def shards(
    inputs,
    upstream,
    master,
    moment_one,
    moment_two,
    hidden_steps,
    key_weight,
    queries,
    key_cache,
    value_cache,
    lengths,
):
    grad_factor = 1.0 / math.sqrt(inputs.shape[0] * lax.axis_size("fsdp") * lax.axis_size("tp"))
    flat = hidden_steps.reshape(16, 5120)
    weight, grad, fresh, attended = learn(
        inputs,
        upstream,
        master,
        moment_one,
        moment_two,
        flat,
        key_weight,
        queries,
        key_cache,
        value_cache,
        lengths,
        grad_factor,
    )
    input_grad, new_master, new_moment = finish(
        upstream, weight.reshape(5120, 1024), grad, master, moment_one, moment_two
    )
    fresh_kv = fresh.reshape(2, 4, 4, 128).transpose(1, 2, 0, 3)
    return (input_grad, new_master, new_moment, fresh_kv, attended)


def solution(mesh):
    in_specs = (
        P(("fsdp", "tp"), None),
        P(("fsdp", "tp"), None),
        P("fsdp", None),
        P("fsdp", None),
        P("fsdp", None),
        P(None, "fsdp", None),
        P(None, "tp"),
        P(None, "fsdp", "tp"),
        P("fsdp", None, "tp"),
        P("fsdp", None, "tp"),
        P("fsdp"),
    )
    out_specs = (
        P(("fsdp", "tp"), None),
        P("fsdp", None),
        P("fsdp", None),
        P(None, "fsdp", None, "tp"),
        P(None, "fsdp", "tp"),
    )
    return jax.shard_map(shards, mesh=mesh, in_specs=in_specs, out_specs=out_specs, check_vma=False)
```

```python
import functools
import math

import jax
import jax.numpy as jnp
from jax import lax
from jax.experimental import pallas as pl
from jax.experimental.pallas import tpu as pltpu
from jax.sharding import PartitionSpec as P

HD = 128
GROUP = 5
MESH = pl.DeviceIdType.MESH


beta_one = 0.9
beta_two = 0.95
learn_rate = 0.004
decay_rate = 0.1
adam_eps = 1e-08
correction_one = 1.0 - 0.9**20
correction_two = 1.0 - 0.95**20

T1, D1, F1, C1, A2, C2, A3, C3 = 0, 8, 16, 24, 27, 39, 42, 45
XS, UT, GX, TP, HS, FR = 48, 52, 53, 54, 62, 78
WZ, WF, WY, WS, SEMS = 94, 96, 98, 106, 114
NT = (((1,), (1,)), ((), ()))

f32, bf16 = jnp.float32, jnp.bfloat16


def adamw(master, grad, moment_one, moment_two):
    new_first = beta_one * moment_one + (1.0 - beta_one) * grad
    new_second = beta_two * moment_two + (1.0 - beta_two) * grad * grad
    update = new_first / correction_one / (jnp.sqrt(new_second / correction_two) + adam_eps)
    return (master - learn_rate * (update + decay_rate * master), new_first)


def learn_kernel(
    grad_factor,
    x_hbm,
    u,
    master_hbm,
    m1_hbm,
    m2_hbm,
    hidden,
    kw_hbm,
    queries,
    k_hbm,
    v_hbm,
    lengths,
    wother,
    gall,
    part_hbm,
    fresh_out,
    attended,
    ut,
    wsame,
    kw,
    keys,
    values,
    qf,
    acc,
    fprob,
    x_own,
    x_sib,
    ut_sib,
    master,
    m1,
    m2,
    ga,
    gc,
    t1,
    r1a,
    r1c,
    s1a,
    s1c,
    r2a,
    r2c,
    s2a,
    s2c,
    r3a,
    r3c,
    gx,
    gt,
    gown,
    wpad,
    hr,
    pf,
    fr,
    ssem,
    rsem,
    lsem,
):
    f, t = lax.axis_index("fsdp"), lax.axis_index("tp")
    z, yl, c = f // 4, (f // 2) % 2, f % 2
    yh, x = t // 4, t % 4
    y = yh * 2 + yl
    sib = (z * 4 + yl * 2 + (1 - c), t)

    def dev_x(d):
        return (f, yh * 4 + (x + d) % 4)

    def dev_y(d):
        yy = (y + d) % 4
        return (z * 4 + (yy % 2) * 2 + c, (yy // 2) * 4 + x)

    def dev_z(d):
        return (((z + d) % 4) * 4 + yl * 2 + c, t)

    def rcopy(src, dst, n, who):
        return pltpu.make_async_remote_copy(
            src_ref=src,
            dst_ref=dst,
            send_sem=ssem.at[n],
            recv_sem=rsem.at[n],
            device_id=who,
            device_id_type=MESH,
        )

    def lanes(zz):
        return pl.ds(pl.multiple_of(zz * 1280, 1280), 1280)

    tcols = pl.ds(pl.multiple_of(t * 128, 128), 128)
    local = [(master_hbm, master)]
    local += [(x_hbm.at[:, lanes((z + k) % 4)], x_own.at[:, lanes((z + k) % 4)]) for k in (1, 2, 3, 4)]
    local += [(kw_hbm, kw), (k_hbm, keys), (v_hbm, values)]
    local += [(m1_hbm.at[:, tcols], m1), (m2_hbm.at[:, tcols], m2)]
    local = [pltpu.make_async_copy(a, b, lsem.at[i]) for i, (a, b) in enumerate(local)]
    for cp in local[:5]:
        cp.start()
    grad_out = pltpu.make_async_copy(gown, gall.at[t], lsem.at[10])

    barrier = pltpu.get_barrier_semaphore()

    @pl.loop(1, 16)
    def _(j):
        pl.semaphore_signal(barrier, 1, device_id=((f + j) % 16, t), device_id_type=MESH)

    @pl.loop(1, 8)
    def _(j):
        pl.semaphore_signal(barrier, 1, device_id=(f, (t + j) % 8), device_id_type=MESH)

    pl.semaphore_signal(
        barrier,
        1,
        device_id=(z * 4 + (1 - yl) * 2 + c, (1 - yh) * 4 + x),
        device_id_type=MESH,
    )

    for tt in range(8):
        block = u[:, tt * 128 : (tt + 1) * 128].T
        place = ((tt % 4) * 2 + tt // 4) * 64
        ut[0, place : place + 64] = block[0:64]
        ut[1, place : place + 64] = block[64:128]
    local[0].wait()
    wsame[z, c] = master[...].astype(bf16)
    pl.semaphore_wait(barrier, 23)

    ut_copy = rcopy(ut.at[1 - c], ut_sib, UT, sib)
    ut_copy.start()
    sib_copies = [
        rcopy(x_hbm.at[:, lanes((z + k) % 4)], x_sib.at[:, lanes((z + k) % 4)], XS + k - 1, sib)
        for k in (1, 2, 3, 4)
    ]
    for cp in sib_copies[:2]:
        cp.start()

    def wz(i):
        piece = wsame.at[z, c]
        return rcopy(piece, piece, WZ + i, dev_z(1 if i == 0 else 3))

    def wf(i):
        piece = wsame.at[(z + (3 if i == 0 else 1)) % 4, c, pl.ds(i * 160, 160)]
        return rcopy(piece, piece, WF + i, dev_z(1 if i == 0 else 3))

    def wy(dz, way):
        zz, rows = (z + dz) % 4, pl.ds(way * 160, 160)
        return rcopy(
            wsame.at[zz, c, rows],
            wother.at[zz, c, rows],
            WY + dz * 2 + way,
            dev_y(1 if way == 0 else 3),
        )

    def ws(dz, other):
        piece = (wother if other else wsame).at[(z + dz) % 4, c]
        return rcopy(piece, piece, WS + other * 4 + dz, sib)

    def part_out(dz):
        zz = (z + dz) % 4
        cols = pl.ds(pl.multiple_of(zz * 640, 640), 640)
        return pltpu.make_async_copy(x_own.at[:, cols], part_hbm.at[zz], lsem.at[11 + dz])

    def input_grad(dz):
        ws(dz, 0).wait()

        @pl.loop(0, 2)
        def _(half):
            zz = (z + dz) % 4
            cols = pl.ds(pl.multiple_of(zz * 640, 640), 640)
            rows = pl.ds(pl.multiple_of(half * 256, 256), 256)
            x_own[rows, cols] = lax.dot_general(
                u[rows], wsame[zz].reshape(640, 1024), NT, preferred_element_type=f32
            ).astype(bf16)

        part_out(dz).start()

    for i in range(2):
        wz(i).start()
    for way in range(2):
        wy(0, way).start()

    def hidden_copy(j):
        to = (f + j) % 16
        cols = pl.ds(pl.multiple_of((to // 2) * 640, 640), 640)
        return rcopy(hidden.at[:, cols], hr.at[j], HS + j, (to, t))

    @pl.loop(1, 16)
    def _(j):
        hidden_copy(j).start()

    hr[0] = hidden[:, pl.ds(pl.multiple_of((f // 2) * 640, 640), 640)]
    wpad[...] = jnp.zeros_like(wpad)

    right, left = (x + 1) % 4, (x + 3) % 4

    def two_hop(i, zz, k):
        return rcopy(
            ga.at[(x + 2) % 4, i, zz], t1.at[i, zz], T1 + i * 4 + k, dev_x(1 if i == 0 else 3)
        )

    def direct(i, zz, k):
        piece = ga.at[right if i == 0 else left, 1 - i, zz]
        return rcopy(piece, r1a.at[i, 1 - i, zz], D1 + i * 4 + k, dev_x(1 if i == 0 else 3))

    def summed(i, zz, k):
        piece = ga.at[right if i == 0 else left, i, zz]
        return rcopy(piece, r1a.at[i, i, zz], F1 + i * 4 + k, dev_x(1 if i == 0 else 3))

    def c1(d):
        return rcopy(gc.at[:, :, (z + d) % 4], r1c.at[d - 1], C1 + d - 1, dev_z(d))

    def a2(d, zz, k):
        yy = (y + d) % 4
        return rcopy(
            s1a.at[yy // 2, zz, yy % 2], r2a.at[d - 1, zz], A2 + (d - 1) * 4 + k, dev_y(d)
        )

    def c2(d):
        return rcopy(s1c.at[(x + d) % 4], r2c.at[d - 1], C2 + d - 1, dev_x(d))

    def a3(d):
        return rcopy(s2a.at[(z + d) % 4], r3a.at[d - 1], A3 + d - 1, dev_z(d))

    def c3(d):
        yy = (y + d) % 4
        return rcopy(s2c.at[yy // 2, yy % 2], r3c.at[d - 1], C3 + d - 1, dev_y(d))

    def pass_on(k):
        zz = (z + 1 + k) % 4
        for i in range(2):
            two_hop(i, zz, k).wait()
            to = right if i == 0 else left

            @pl.loop(0, 2)
            def _(ll):
                got = ga[to, i, zz, ll].astype(f32) + t1[i, zz, ll].astype(f32)
                ga[to, i, zz, ll] = got.astype(bf16)

            summed(i, zz, k).start()

    ut_copy.wait()
    for k in range(4):
        zz = (z + 1 + k) % 4
        local[1 + k].wait()
        sib_copies[k].wait()
        if k < 2:
            sib_copies[k + 2].start()

        @pl.loop(0, 4)
        def _(i):
            ll, half = i // 2, i % 2
            cols = pl.ds(pl.multiple_of(zz * 1280 + ll * 640, 640), 640)
            rows = pl.ds(pl.multiple_of(half * 256, 256), 256)
            part = jnp.dot(ut[c, rows], x_own[:, cols], preferred_element_type=f32)
            part += jnp.dot(ut_sib[rows], x_sib[:, cols], preferred_element_type=f32)
            part = part.astype(bf16)
            for b in range(4):
                xx, hh = half * 2 + b // 2, b % 2
                ga[xx, hh, zz, ll] = part[b * 64 : (b + 1) * 64, 0:512]
                gc[xx, hh, zz, ll] = part[b * 64 : (b + 1) * 64, 512:640]

        for i in range(2):
            two_hop(i, zz, k).start()
        for i in range(2):
            direct(i, zz, k).start()
        if k < 3:
            c1(k + 1).start()
        if k > 0:
            pass_on(k - 1)
        if k == 1:
            for cp in local[5:]:
                cp.start()
            ws(0, 0).start()
    pass_on(3)

    for i in range(2):
        wz(i).wait()
    for i in range(2):
        wf(i).start()
    for dz in (1, 3):
        for way in range(2):
            wy(dz, way).start()
        ws(dz, 0).start()

    local[5].wait()
    fresh_out[0] = jnp.dot(hidden[...], kw[...], preferred_element_type=f32).astype(bf16)
    qf[...] = jnp.zeros_like(qf)
    for step in range(4):
        for g in range(GROUP):
            qf[:, step * GROUP + g] = queries[step, :, g * HD : (g + 1) * HD].astype(f32)
    local[6].wait()
    local[7].wait()
    scale = 1.0 / math.sqrt(HD)

    def attend(r):
        q = qf[r].astype(bf16)
        scores = lax.dot_general(q, keys[r], NT, preferred_element_type=f32) * scale
        slots = lax.broadcasted_iota(jnp.int32, (32, 4096), 1)
        scores = jnp.where(slots < lengths[r], scores, -1e30)
        extra = lax.dot_general(q, fresh_out[0], NT, preferred_element_type=f32) * scale
        line = lax.broadcasted_iota(jnp.int32, (32, 16), 0)
        item = lax.broadcasted_iota(jnp.int32, (32, 16), 1)
        seen = ((item & 3) == r) & ((item >> 2) * GROUP <= line)
        extra = jnp.where(seen, extra, -1e30)
        highest = jnp.maximum(
            jnp.max(scores, axis=1, keepdims=True), jnp.max(extra, axis=1, keepdims=True)
        )
        scores = jnp.exp(scores - highest)
        extra = jnp.exp(extra - highest)
        norm = 1.0 / (
            jnp.sum(scores, axis=1, keepdims=True) + jnp.sum(extra, axis=1, keepdims=True)
        )
        fprob[r] = (extra * norm).astype(bf16)
        acc[r] = jnp.dot((scores * norm).astype(bf16), values[r], preferred_element_type=f32)

    def total(own, others, index, count=3):
        got = own.astype(f32)
        for d in range(count):
            got += others[(d,) + index].astype(f32)
        return got

    def first(k):
        zz = (z + 1 + k) % 4
        for i in range(2):
            direct(i, zz, k).wait()
            summed(i, zz, k).wait()

        @pl.loop(0, 4)
        def _(i):
            hh, ll = i // 2, i % 2
            s1a[hh, zz, ll] = total(ga[x, hh, zz, ll], r1a, (hh, zz, ll), 2).astype(bf16)

        for d in (2, 1, 3):
            a2(d, zz, k).start()

    def second(k):
        zz = (z + 1 + k) % 4
        for d in (1, 2, 3):
            a2(d, zz, k).wait()
        s2a[zz] = total(s1a[yh, zz, yl], r2a, (zz,))
        if k < 3:
            a3(k + 1).start()

    first(0)
    pl.loop(0, 2)(attend)
    for d in (1, 2, 3):
        c1(d).wait()

    @pl.loop(0, 16)
    def _(i):
        xx, hh, ll = i // 4, (i // 2) % 2, i % 2
        s1c[xx, hh, ll] = total(gc[xx, hh, z, ll], r1c, (xx, hh, ll)).astype(bf16)

    for d in (2, 1, 3):
        c2(d).start()
    first(1)
    pl.loop(2, 4)(attend)
    for i in range(2):
        wf(i).wait()
    for way in range(2):
        wy(2, way).start()
    ws(2, 0).start()
    second(0)
    first(2)
    input_grad(0)
    second(1)
    for d in (1, 2, 3):
        c2(d).wait()

    @pl.loop(0, 4)
    def _(i):
        hh, ll = i // 2, i % 2
        s2c[hh, ll] = total(s1c[x, hh, ll], r2c, (hh, ll))

    for d in (2, 1, 3):
        c3(d).start()
    for way in range(2):
        wy(0, way).wait()
    ws(0, 1).start()
    first(3)
    second(2)
    input_grad(1)
    second(3)

    for d in (1, 2, 3):
        a3(d).wait()
        c3(d).wait()
    gx[c, :, 0:512] = total(s2a[z], r3a, ()) * grad_factor
    gx[c, :, 512:640] = total(s2c[yh, yl], r3c, ()) * grad_factor
    gx_copy = rcopy(gx.at[c], gx.at[c], GX, sib)
    gx_copy.start()
    gx_copy.wait()
    gt[...] = gx[...].reshape(128, 640).T
    mine = pl.ds(pl.multiple_of(c * 320, 320), 320)
    gown[...] = gt[mine, :].astype(bf16)
    grad_out.start()

    def tp_copy(j):
        return rcopy(gown, gall.at[t], TP + j, (f, (t + j) % 8))

    @pl.loop(1, 8)
    def _(j):
        tp_copy(j).start()

    local[8].wait()
    local[9].wait()
    stepped, _ = adamw(master[:, tcols], gown[...].astype(f32), m1[...], m2[...])
    wpad[mine, :] = stepped.astype(bf16)

    @pl.loop(1, 16)
    def _(j):
        hidden_copy(j).wait()

    pf[...] = jnp.dot(
        hr[...].reshape(256, 640), wpad[...], preferred_element_type=f32
    ).reshape(16, 16, 128)

    def fresh_copy(j):
        return rcopy(pf.at[j], fr.at[j], FR + j, ((f + 16 - j) % 16, t))

    @pl.loop(1, 16)
    def _(j):
        fresh_copy(j).start()

    for dz in (1, 3, 2):
        for way in range(2):
            wy(dz, way).wait()
        ws(dz, 1).start()
    input_grad(3)
    input_grad(2)

    @pl.loop(1, 16)
    def _(j):
        fresh_copy(j).wait()

    fr[0] = pf[0]
    fresh_out[1] = jnp.sum(fr[...], axis=0).astype(bf16)

    @pl.loop(0, 4)
    def _(r):
        acc[r] += jnp.dot(fprob[r], fresh_out[1], preferred_element_type=f32)

    for step in range(4):
        for g in range(GROUP):
            attended[step, :, g * HD : (g + 1) * HD] = acc[:, step * GROUP + g].astype(bf16)

    grad_out.wait()

    @pl.loop(1, 8)
    def _(j):
        tp_copy(j).wait()

    for dz in range(4):
        ws(dz, 1).wait()
        part_out(dz).wait()


def learn(
    inputs, upstream, master, m1, m2, flat, key_weight, queries, keys, values, lengths, grad_factor
):
    hbm = pl.BlockSpec(memory_space=pl.ANY)
    vmem = pl.BlockSpec(memory_space=pltpu.VMEM)
    smem = pl.BlockSpec(memory_space=pltpu.SMEM)
    shape = jax.ShapeDtypeStruct
    V = pltpu.VMEM
    scratch = [
        V((2, 512, 512), bf16),
        V((4, 2, 320, 1024), bf16),
        V((5120, 128), bf16),
        V((4, 4096, 128), bf16),
        V((4, 4096, 128), bf16),
        V((4, 32, 128), f32),
        V((4, 32, 128), f32),
        V((4, 32, 16), bf16),
        V((512, 5120), bf16),
        V((512, 5120), bf16),
        V((512, 512), bf16),
        V((320, 1024), f32),
        V((320, 128), f32),
        V((320, 128), f32),
        V((4, 2, 4, 2, 64, 512), bf16),
        V((4, 2, 4, 2, 64, 128), bf16),
        V((2, 4, 2, 64, 512), bf16),
        V((2, 2, 4, 2, 64, 512), bf16),
        V((3, 4, 2, 2, 64, 128), bf16),
        V((2, 4, 2, 64, 512), bf16),
        V((4, 2, 2, 64, 128), bf16),
        V((3, 4, 64, 512), bf16),
        V((3, 2, 2, 64, 128), bf16),
        V((4, 64, 512), f32),
        V((2, 2, 64, 128), f32),
        V((3, 64, 512), f32),
        V((3, 64, 128), f32),
        V((2, 64, 640), f32),
        V((640, 128), f32),
        V((320, 128), bf16),
        V((640, 128), bf16),
        V((16, 16, 640), bf16),
        V((16, 16, 128), f32),
        V((16, 16, 128), f32),
        pltpu.SemaphoreType.DMA((SEMS,)),
        pltpu.SemaphoreType.DMA((SEMS,)),
        pltpu.SemaphoreType.DMA((15,)),
    ]
    return pl.pallas_call(
        functools.partial(learn_kernel, grad_factor),
        out_shape=(
            shape((4, 2, 320, 1024), bf16),
            shape((8, 320, 128), bf16),
            shape((4, 512, 640), bf16),
            shape((2, 16, 128), bf16),
            shape((4, 4, 640), bf16),
        ),
        in_specs=[hbm, vmem, hbm, hbm, hbm, vmem, hbm, vmem, hbm, hbm, smem],
        out_specs=[hbm, hbm, hbm, vmem, vmem],
        scratch_shapes=scratch,
        name="learn",
        compiler_params=pltpu.CompilerParams(
            collective_id=0, has_side_effects=True, vmem_limit_bytes=56 << 20
        ),
    )(inputs, upstream, master, m1, m2, flat, key_weight, queries, keys, values, lengths)


def finish_kernel(u, part, w, grad, master, m1, m2, input_grad, new_master, new_moment):
    yl = (lax.axis_index("fsdp") // 2) % 2
    same = pl.ds(pl.multiple_of(yl * 640, 640), 640)
    other = pl.ds(pl.multiple_of((1 - yl) * 640, 640), 640)
    input_grad[:, same] = part[...]
    input_grad[:, other] = lax.dot_general(
        u[...], w[...], NT, preferred_element_type=f32
    ).astype(bf16)
    for i in range(2):
        cols = slice(i * 128, (i + 1) * 128)
        new_master[:, cols], new_moment[:, cols] = adamw(
            master[:, cols], grad[i].astype(f32), m1[:, cols], m2[:, cols]
        )


def finish(upstream, part, weight, grad, master, m1, m2):
    cols = pl.BlockSpec((320, 256), lambda i: (0, i))
    return pl.pallas_call(
        finish_kernel,
        grid=(4,),
        out_shape=(
            jax.ShapeDtypeStruct((512, 5120), bf16),
            jax.ShapeDtypeStruct((320, 1024), f32),
            jax.ShapeDtypeStruct((320, 1024), f32),
        ),
        in_specs=[
            pl.BlockSpec((512, 1024), lambda i: (0, 0)),
            pl.BlockSpec((None, 512, 640), lambda i: (i, 0, 0)),
            pl.BlockSpec((640, 1024), lambda i: (i, 0)),
            pl.BlockSpec((2, 320, 128), lambda i: (i, 0, 0)),
            cols,
            cols,
            cols,
        ],
        out_specs=[pl.BlockSpec((512, 1280), lambda i: (0, i)), cols, cols],
        name="finish",
        compiler_params=pltpu.CompilerParams(vmem_limit_bytes=60 << 20),
    )(upstream, part, weight, grad, master, m1, m2)


def shards(
    inputs,
    upstream,
    master,
    moment_one,
    moment_two,
    hidden_steps,
    key_weight,
    queries,
    key_cache,
    value_cache,
    lengths,
):
    grad_factor = 1.0 / math.sqrt(inputs.shape[0] * lax.axis_size("fsdp") * lax.axis_size("tp"))
    flat = hidden_steps.reshape(16, 5120)
    weight, grad, part, fresh, attended = learn(
        inputs,
        upstream,
        master,
        moment_one,
        moment_two,
        flat,
        key_weight,
        queries,
        key_cache,
        value_cache,
        lengths,
        grad_factor,
    )
    input_grad, new_master, new_moment = finish(
        upstream, part, weight.reshape(2560, 1024), grad, master, moment_one, moment_two
    )
    fresh_kv = fresh.reshape(2, 4, 4, 128).transpose(1, 2, 0, 3)
    return (input_grad, new_master, new_moment, fresh_kv, attended)


def solution(mesh):
    in_specs = (
        P(("fsdp", "tp"), None),
        P(("fsdp", "tp"), None),
        P("fsdp", None),
        P("fsdp", None),
        P("fsdp", None),
        P(None, "fsdp", None),
        P(None, "tp"),
        P(None, "fsdp", "tp"),
        P("fsdp", None, "tp"),
        P("fsdp", None, "tp"),
        P("fsdp"),
    )
    out_specs = (
        P(("fsdp", "tp"), None),
        P("fsdp", None),
        P("fsdp", None),
        P(None, "fsdp", None, "tp"),
        P(None, "fsdp", "tp"),
    )
    return jax.shard_map(shards, mesh=mesh, in_specs=in_specs, out_specs=out_specs, check_vma=False)
```

```python
import functools
import math

import jax
import jax.numpy as jnp
from jax import lax
from jax.experimental import pallas as pl
from jax.experimental.pallas import tpu as pltpu
from jax.sharding import PartitionSpec as P

HD = 128
GROUP = 5
MESH = pl.DeviceIdType.MESH


beta_one = 0.9
beta_two = 0.95
learn_rate = 0.004
decay_rate = 0.1
adam_eps = 1e-08
correction_one = 1.0 - 0.9**20
correction_two = 1.0 - 0.95**20

T1, D1, F1, C1, A2, C2, A3, C3 = 0, 8, 16, 24, 27, 39, 42, 45
XS, UT, GX, TP, HS, FR = 48, 52, 53, 54, 62, 78
WZ, WF, WY, WS, WX, B1, B2, B3, SEMS = 94, 96, 98, 114, 122, 134, 146, 149, 152
WHOLE, QUARTER = 192, 32
NT = (((1,), (1,)), ((), ()))

f32, bf16 = jnp.float32, jnp.bfloat16


def adamw(master, grad, moment_one, moment_two):
    new_first = beta_one * moment_one + (1.0 - beta_one) * grad
    new_second = beta_two * moment_two + (1.0 - beta_two) * grad * grad
    update = new_first / correction_one / (jnp.sqrt(new_second / correction_two) + adam_eps)
    return (master - learn_rate * (update + decay_rate * master), new_first)


def learn_kernel(
    grad_factor,
    x_hbm,
    u,
    master_hbm,
    m1_hbm,
    m2_hbm,
    hidden,
    kw_hbm,
    queries,
    k_hbm,
    v_hbm,
    lengths,
    wother,
    gall,
    part_hbm,
    fresh_out,
    attended,
    ut,
    wsame,
    kw,
    keys,
    values,
    qf,
    acc,
    fprob,
    x_own,
    x_sib,
    ut_sib,
    master,
    m1,
    m2,
    ga,
    gb,
    gc,
    t1,
    r1a,
    r1b,
    r1c,
    s1a,
    s1b,
    s1c,
    r2a,
    r2b,
    r2c,
    s2a,
    s2b,
    s2c,
    r3a,
    r3b,
    r3c,
    gx,
    gt,
    gown,
    wpad,
    hr,
    pf,
    fr,
    ssem,
    rsem,
    lsem,
):
    f, t = lax.axis_index("fsdp"), lax.axis_index("tp")
    z, yl, c = f // 4, (f // 2) % 2, f % 2
    yh, x = t // 4, t % 4
    y = yh * 2 + yl
    sib = (z * 4 + yl * 2 + (1 - c), t)

    def dev_x(d):
        return (f, yh * 4 + (x + d) % 4)

    def dev_y(d):
        yy = (y + d) % 4
        return (z * 4 + (yy % 2) * 2 + c, (yy // 2) * 4 + x)

    def dev_z(d):
        return (((z + d) % 4) * 4 + yl * 2 + c, t)

    def rcopy(src, dst, n, who):
        return pltpu.make_async_remote_copy(
            src_ref=src,
            dst_ref=dst,
            send_sem=ssem.at[n],
            recv_sem=rsem.at[n],
            device_id=who,
            device_id_type=MESH,
        )

    def lanes(zz):
        return pl.ds(pl.multiple_of(zz * 1280, 1280), 1280)

    tcols = pl.ds(pl.multiple_of(t * 128, 128), 128)
    local = [(master_hbm, master)]
    local += [(x_hbm.at[:, lanes((z + k) % 4)], x_own.at[:, lanes((z + k) % 4)]) for k in (1, 2, 3, 4)]
    local += [(kw_hbm, kw), (k_hbm, keys), (v_hbm, values)]
    local += [(m1_hbm.at[:, tcols], m1), (m2_hbm.at[:, tcols], m2)]
    local = [pltpu.make_async_copy(a, b, lsem.at[i]) for i, (a, b) in enumerate(local)]
    for cp in local[:5]:
        cp.start()
    grad_out = pltpu.make_async_copy(gown, gall.at[t], lsem.at[10])

    barrier = pltpu.get_barrier_semaphore()

    @pl.loop(1, 16)
    def _(j):
        pl.semaphore_signal(barrier, 1, device_id=((f + j) % 16, t), device_id_type=MESH)

    @pl.loop(1, 8)
    def _(j):
        pl.semaphore_signal(barrier, 1, device_id=(f, (t + j) % 8), device_id_type=MESH)

    pl.semaphore_signal(
        barrier,
        1,
        device_id=(z * 4 + (1 - yl) * 2 + c, (1 - yh) * 4 + x),
        device_id_type=MESH,
    )

    for tt in range(8):
        block = u[:, tt * 128 : (tt + 1) * 128].T
        place = ((tt % 4) * 2 + tt // 4) * 64
        ut[0, place : place + 64] = block[0:64]
        ut[1, place : place + 64] = block[64:128]
    local[0].wait()
    wsame[z, c] = master[...].astype(bf16)
    pl.semaphore_wait(barrier, 23)

    ut_copy = rcopy(ut.at[1 - c], ut_sib, UT, sib)
    ut_copy.start()
    sib_copies = [
        rcopy(x_hbm.at[:, lanes((z + k) % 4)], x_sib.at[:, lanes((z + k) % 4)], XS + k - 1, sib)
        for k in (1, 2, 3, 4)
    ]
    for cp in sib_copies[:2]:
        cp.start()

    quarter = WHOLE + x * QUARTER

    def wz(i):
        piece = wsame.at[z, c]
        return rcopy(piece, piece, WZ + i, dev_z(1 if i == 0 else 3))

    def wf(i):
        piece = wsame.at[(z + (3 if i == 0 else 1)) % 4, c, pl.ds(i * 160, 160)]
        return rcopy(piece, piece, WF + i, dev_z(1 if i == 0 else 3))

    def wy(dz, way, part):
        zz = (z + dz) % 4
        first = (way * (WHOLE // 2), pl.multiple_of(quarter + way * (QUARTER // 2), 16))[part]
        rows = pl.ds(first, (WHOLE // 2, QUARTER // 2)[part])
        return rcopy(
            wsame.at[zz, c, rows],
            wother.at[zz, c, rows],
            WY + (dz * 2 + way) * 2 + part,
            dev_y(1 if way == 0 else 3),
        )

    def wx(dz, d):
        piece = wother.at[(z + dz) % 4, c, pl.ds(pl.multiple_of(quarter, 32), QUARTER)]
        return rcopy(piece, piece, WX + dz * 3 + d - 1, dev_x(d))

    def wy_start(dz):
        for way in range(2):
            for part in range(2):
                wy(dz, way, part).start()

    def spread(dz):
        for way in range(2):
            for part in range(2):
                wy(dz, way, part).wait()
        for d in (2, 1, 3):
            wx(dz, d).start()

    def arrived(dz):
        for d in (1, 2, 3):
            wx(dz, d).wait()
        ws(dz, 1).start()

    def ws(dz, other):
        piece = (wother if other else wsame).at[(z + dz) % 4, c]
        return rcopy(piece, piece, WS + other * 4 + dz, sib)

    def part_out(dz):
        zz = (z + dz) % 4
        cols = pl.ds(pl.multiple_of(zz * 640, 640), 640)
        return pltpu.make_async_copy(x_own.at[:, cols], part_hbm.at[zz], lsem.at[11 + dz])

    def input_grad(dz):
        ws(dz, 0).wait()

        @pl.loop(0, 2)
        def _(half):
            zz = (z + dz) % 4
            cols = pl.ds(pl.multiple_of(zz * 640, 640), 640)
            rows = pl.ds(pl.multiple_of(half * 256, 256), 256)
            x_own[rows, cols] = lax.dot_general(
                u[rows], wsame[zz].reshape(640, 1024), NT, preferred_element_type=f32
            ).astype(bf16)

        part_out(dz).start()

    for i in range(2):
        wz(i).start()
    wy_start(0)

    def hidden_copy(j):
        to = (f + j) % 16
        cols = pl.ds(pl.multiple_of((to // 2) * 640, 640), 640)
        return rcopy(hidden.at[:, cols], hr.at[j], HS + j, (to, t))

    @pl.loop(1, 16)
    def _(j):
        hidden_copy(j).start()

    hr[0] = hidden[:, pl.ds(pl.multiple_of((f // 2) * 640, 640), 640)]
    wpad[...] = jnp.zeros_like(wpad)

    right, left = (x + 1) % 4, (x + 3) % 4

    def two_hop(i, zz, k):
        return rcopy(
            ga.at[(x + 2) % 4, i, zz], t1.at[i, zz], T1 + i * 4 + k, dev_x(1 if i == 0 else 3)
        )

    def direct(i, zz, k):
        piece = ga.at[right if i == 0 else left, 1 - i, zz]
        return rcopy(piece, r1a.at[i, 1 - i, zz], D1 + i * 4 + k, dev_x(1 if i == 0 else 3))

    def summed(i, zz, k):
        piece = ga.at[right if i == 0 else left, i, zz]
        return rcopy(piece, r1a.at[i, i, zz], F1 + i * 4 + k, dev_x(1 if i == 0 else 3))

    def b1(d, zz, k):
        yy = (y + d) % 4
        return rcopy(
            gb.at[:, yy // 2, zz, yy % 2], r1b.at[d - 1, :, zz], B1 + (d - 1) * 4 + k, dev_y(d)
        )

    def b2(d):
        return rcopy(s1b.at[:, (z + d) % 4], r2b.at[d - 1], B2 + d - 1, dev_z(d))

    def b3(d):
        return rcopy(s2b.at[(x + d) % 4], r3b.at[d - 1], B3 + d - 1, dev_x(d))

    def c1(d):
        return rcopy(gc.at[:, :, (z + d) % 4], r1c.at[d - 1], C1 + d - 1, dev_z(d))

    def a2(d, zz, k):
        yy = (y + d) % 4
        return rcopy(
            s1a.at[yy // 2, zz, yy % 2], r2a.at[d - 1, zz], A2 + (d - 1) * 4 + k, dev_y(d)
        )

    def c2(d):
        return rcopy(s1c.at[(x + d) % 4], r2c.at[d - 1], C2 + d - 1, dev_x(d))

    def a3(d):
        return rcopy(s2a.at[(z + d) % 4], r3a.at[d - 1], A3 + d - 1, dev_z(d))

    def c3(d):
        yy = (y + d) % 4
        return rcopy(s2c.at[yy // 2, yy % 2], r3c.at[d - 1], C3 + d - 1, dev_y(d))

    def pass_on(k):
        zz = (z + 1 + k) % 4
        for i in range(2):
            two_hop(i, zz, k).wait()
            to = right if i == 0 else left

            @pl.loop(0, 2)
            def _(ll):
                got = ga[to, i, zz, ll].astype(f32) + t1[i, zz, ll].astype(f32)
                ga[to, i, zz, ll] = got.astype(bf16)

            summed(i, zz, k).start()

    ut_copy.wait()
    for k in range(4):
        zz = (z + 1 + k) % 4
        local[1 + k].wait()
        sib_copies[k].wait()
        if k < 2:
            sib_copies[k + 2].start()

        @pl.loop(0, 4)
        def _(i):
            ll, half = i // 2, i % 2
            cols = pl.ds(pl.multiple_of(zz * 1280 + ll * 640, 640), 640)
            rows = pl.ds(pl.multiple_of(half * 256, 256), 256)
            part = jnp.dot(ut[c, rows], x_own[:, cols], preferred_element_type=f32)
            part += jnp.dot(ut_sib[rows], x_sib[:, cols], preferred_element_type=f32)
            part = part.astype(bf16)
            for b in range(4):
                xx, hh = half * 2 + b // 2, b % 2
                ga[xx, hh, zz, ll] = part[b * 64 : (b + 1) * 64, 0:384]
                gb[xx, hh, zz, ll] = part[b * 64 : (b + 1) * 64, 384:512]
                gc[xx, hh, zz, ll] = part[b * 64 : (b + 1) * 64, 512:640]

        for i in range(2):
            two_hop(i, zz, k).start()
        for i in range(2):
            direct(i, zz, k).start()
        for d in (2, 1, 3):
            b1(d, zz, k).start()
        if k < 3:
            c1(k + 1).start()
        if k > 0:
            pass_on(k - 1)
        if k == 1:
            for cp in local[5:]:
                cp.start()
            ws(0, 0).start()
    pass_on(3)

    for i in range(2):
        wz(i).wait()
    for i in range(2):
        wf(i).start()
    for dz in (1, 3):
        wy_start(dz)
        ws(dz, 0).start()

    local[5].wait()
    fresh_out[0] = jnp.dot(hidden[...], kw[...], preferred_element_type=f32).astype(bf16)
    qf[...] = jnp.zeros_like(qf)
    for step in range(4):
        for g in range(GROUP):
            qf[:, step * GROUP + g] = queries[step, :, g * HD : (g + 1) * HD].astype(f32)
    local[6].wait()
    local[7].wait()
    scale = 1.0 / math.sqrt(HD)

    def attend(r):
        q = qf[r].astype(bf16)
        scores = lax.dot_general(q, keys[r], NT, preferred_element_type=f32) * scale
        slots = lax.broadcasted_iota(jnp.int32, (32, 4096), 1)
        scores = jnp.where(slots < lengths[r], scores, -1e30)
        extra = lax.dot_general(q, fresh_out[0], NT, preferred_element_type=f32) * scale
        line = lax.broadcasted_iota(jnp.int32, (32, 16), 0)
        item = lax.broadcasted_iota(jnp.int32, (32, 16), 1)
        seen = ((item & 3) == r) & ((item >> 2) * GROUP <= line)
        extra = jnp.where(seen, extra, -1e30)
        highest = jnp.maximum(
            jnp.max(scores, axis=1, keepdims=True), jnp.max(extra, axis=1, keepdims=True)
        )
        scores = jnp.exp(scores - highest)
        extra = jnp.exp(extra - highest)
        norm = 1.0 / (
            jnp.sum(scores, axis=1, keepdims=True) + jnp.sum(extra, axis=1, keepdims=True)
        )
        fprob[r] = (extra * norm).astype(bf16)
        acc[r] = jnp.dot((scores * norm).astype(bf16), values[r], preferred_element_type=f32)

    def total(own, others, index, count=3):
        got = own.astype(f32)
        for d in range(count):
            got += others[(d,) + index].astype(f32)
        return got

    def first(k):
        zz = (z + 1 + k) % 4
        for i in range(2):
            direct(i, zz, k).wait()
            summed(i, zz, k).wait()

        @pl.loop(0, 4)
        def _(i):
            hh, ll = i // 2, i % 2
            s1a[hh, zz, ll] = total(ga[x, hh, zz, ll], r1a, (hh, zz, ll), 2).astype(bf16)

        for d in (2, 1, 3):
            a2(d, zz, k).start()

    def second(k):
        zz = (z + 1 + k) % 4
        for d in (1, 2, 3):
            a2(d, zz, k).wait()
        s2a[zz] = total(s1a[yh, zz, yl], r2a, (zz,))
        if k < 3:
            a3(k + 1).start()

    def first_b(k):
        zz = (z + 1 + k) % 4
        for d in (1, 2, 3):
            b1(d, zz, k).wait()

        @pl.loop(0, 4)
        def _(i):
            s1b[i, zz] = total(gb[i, yh, zz, yl], r1b, (i, zz)).astype(bf16)

        if k < 3:
            b2(k + 1).start()

    first(0)
    first_b(0)
    pl.loop(0, 2)(attend)
    spread(0)
    first(1)
    first_b(1)
    for d in (1, 2, 3):
        c1(d).wait()

    @pl.loop(0, 16)
    def _(i):
        xx, hh, ll = i // 4, (i // 2) % 2, i % 2
        s1c[xx, hh, ll] = total(gc[xx, hh, z, ll], r1c, (xx, hh, ll)).astype(bf16)

    for d in (2, 1, 3):
        c2(d).start()
    for i in range(2):
        wf(i).wait()
    wy_start(2)
    ws(2, 0).start()
    pl.loop(2, 4)(attend)
    first(2)
    first_b(2)
    second(0)
    input_grad(0)
    first(3)
    first_b(3)
    second(1)
    for d in (1, 2, 3):
        c2(d).wait()

    @pl.loop(0, 4)
    def _(i):
        hh, ll = i // 2, i % 2
        s2c[hh, ll] = total(s1c[x, hh, ll], r2c, (hh, ll))

    for d in (2, 1, 3):
        c3(d).start()
    for d in (1, 2, 3):
        b2(d).wait()

    @pl.loop(0, 4)
    def _(i):
        s2b[i] = total(s1b[i, z], r2b, (i,))

    for d in (2, 1, 3):
        b3(d).start()
    spread(1)
    spread(3)
    second(2)
    second(3)

    for d in (1, 2, 3):
        a3(d).wait()
        b3(d).wait()
        c3(d).wait()
    gx[c, :, 0:384] = total(s2a[z], r3a, ()) * grad_factor
    gx[c, :, 384:512] = total(s2b[x], r3b, ()) * grad_factor
    gx[c, :, 512:640] = total(s2c[yh, yl], r3c, ()) * grad_factor
    gx_copy = rcopy(gx.at[c], gx.at[c], GX, sib)
    gx_copy.start()
    gx_copy.wait()
    gt[...] = gx[...].reshape(128, 640).T
    mine = pl.ds(pl.multiple_of(c * 320, 320), 320)
    gown[...] = gt[mine, :].astype(bf16)
    grad_out.start()

    def tp_copy(j):
        return rcopy(gown, gall.at[t], TP + j, (f, (t + j) % 8))

    @pl.loop(1, 8)
    def _(j):
        tp_copy(j).start()

    local[8].wait()
    local[9].wait()
    stepped, _ = adamw(master[:, tcols], gown[...].astype(f32), m1[...], m2[...])
    wpad[mine, :] = stepped.astype(bf16)

    @pl.loop(1, 16)
    def _(j):
        hidden_copy(j).wait()

    pf[...] = jnp.dot(
        hr[...].reshape(256, 640), wpad[...], preferred_element_type=f32
    ).reshape(16, 16, 128)

    def fresh_copy(j):
        return rcopy(pf.at[j], fr.at[j], FR + j, ((f + 16 - j) % 16, t))

    @pl.loop(1, 16)
    def _(j):
        fresh_copy(j).start()

    spread(2)
    for dz in (0, 1, 3):
        arrived(dz)
    input_grad(1)
    input_grad(3)
    input_grad(2)
    arrived(2)

    @pl.loop(1, 16)
    def _(j):
        fresh_copy(j).wait()

    fr[0] = pf[0]
    fresh_out[1] = jnp.sum(fr[...], axis=0).astype(bf16)

    @pl.loop(0, 4)
    def _(r):
        acc[r] += jnp.dot(fprob[r], fresh_out[1], preferred_element_type=f32)

    for step in range(4):
        for g in range(GROUP):
            attended[step, :, g * HD : (g + 1) * HD] = acc[:, step * GROUP + g].astype(bf16)

    grad_out.wait()

    @pl.loop(1, 8)
    def _(j):
        tp_copy(j).wait()

    for dz in range(4):
        ws(dz, 1).wait()
        part_out(dz).wait()


def learn(
    inputs, upstream, master, m1, m2, flat, key_weight, queries, keys, values, lengths, grad_factor
):
    hbm = pl.BlockSpec(memory_space=pl.ANY)
    vmem = pl.BlockSpec(memory_space=pltpu.VMEM)
    smem = pl.BlockSpec(memory_space=pltpu.SMEM)
    shape = jax.ShapeDtypeStruct
    V = pltpu.VMEM
    scratch = [
        V((2, 512, 512), bf16),
        V((4, 2, 320, 1024), bf16),
        V((5120, 128), bf16),
        V((4, 4096, 128), bf16),
        V((4, 4096, 128), bf16),
        V((4, 32, 128), f32),
        V((4, 32, 128), f32),
        V((4, 32, 16), bf16),
        V((512, 5120), bf16),
        V((512, 5120), bf16),
        V((512, 512), bf16),
        V((320, 1024), f32),
        V((320, 128), f32),
        V((320, 128), f32),
        V((4, 2, 4, 2, 64, 384), bf16),
        V((4, 2, 4, 2, 64, 128), bf16),
        V((4, 2, 4, 2, 64, 128), bf16),
        V((2, 4, 2, 64, 384), bf16),
        V((2, 2, 4, 2, 64, 384), bf16),
        V((3, 4, 4, 64, 128), bf16),
        V((3, 4, 2, 2, 64, 128), bf16),
        V((2, 4, 2, 64, 384), bf16),
        V((4, 4, 64, 128), bf16),
        V((4, 2, 2, 64, 128), bf16),
        V((3, 4, 64, 384), bf16),
        V((3, 4, 64, 128), bf16),
        V((3, 2, 2, 64, 128), bf16),
        V((4, 64, 384), f32),
        V((4, 64, 128), f32),
        V((2, 2, 64, 128), f32),
        V((3, 64, 384), f32),
        V((3, 64, 128), f32),
        V((3, 64, 128), f32),
        V((2, 64, 640), f32),
        V((640, 128), f32),
        V((320, 128), bf16),
        V((640, 128), bf16),
        V((16, 16, 640), bf16),
        V((16, 16, 128), f32),
        V((16, 16, 128), f32),
        pltpu.SemaphoreType.DMA((SEMS,)),
        pltpu.SemaphoreType.DMA((SEMS,)),
        pltpu.SemaphoreType.DMA((15,)),
    ]
    return pl.pallas_call(
        functools.partial(learn_kernel, grad_factor),
        out_shape=(
            shape((4, 2, 320, 1024), bf16),
            shape((8, 320, 128), bf16),
            shape((4, 512, 640), bf16),
            shape((2, 16, 128), bf16),
            shape((4, 4, 640), bf16),
        ),
        in_specs=[hbm, vmem, hbm, hbm, hbm, vmem, hbm, vmem, hbm, hbm, smem],
        out_specs=[hbm, hbm, hbm, vmem, vmem],
        scratch_shapes=scratch,
        name="learn",
        compiler_params=pltpu.CompilerParams(
            collective_id=0, has_side_effects=True, vmem_limit_bytes=56 << 20
        ),
    )(inputs, upstream, master, m1, m2, flat, key_weight, queries, keys, values, lengths)


def finish_kernel(u, part, w, grad, master, m1, m2, input_grad, new_master, new_moment):
    yl = (lax.axis_index("fsdp") // 2) % 2
    same = pl.ds(pl.multiple_of(yl * 640, 640), 640)
    other = pl.ds(pl.multiple_of((1 - yl) * 640, 640), 640)
    input_grad[:, same] = part[...]
    input_grad[:, other] = lax.dot_general(
        u[...], w[...], NT, preferred_element_type=f32
    ).astype(bf16)
    for i in range(2):
        cols = slice(i * 128, (i + 1) * 128)
        new_master[:, cols], new_moment[:, cols] = adamw(
            master[:, cols], grad[i].astype(f32), m1[:, cols], m2[:, cols]
        )


def finish(upstream, part, weight, grad, master, m1, m2):
    cols = pl.BlockSpec((320, 256), lambda i: (0, i))
    return pl.pallas_call(
        finish_kernel,
        grid=(4,),
        out_shape=(
            jax.ShapeDtypeStruct((512, 5120), bf16),
            jax.ShapeDtypeStruct((320, 1024), f32),
            jax.ShapeDtypeStruct((320, 1024), f32),
        ),
        in_specs=[
            pl.BlockSpec((512, 1024), lambda i: (0, 0)),
            pl.BlockSpec((None, 512, 640), lambda i: (i, 0, 0)),
            pl.BlockSpec((640, 1024), lambda i: (i, 0)),
            pl.BlockSpec((2, 320, 128), lambda i: (i, 0, 0)),
            cols,
            cols,
            cols,
        ],
        out_specs=[pl.BlockSpec((512, 1280), lambda i: (0, i)), cols, cols],
        name="finish",
        compiler_params=pltpu.CompilerParams(vmem_limit_bytes=60 << 20),
    )(upstream, part, weight, grad, master, m1, m2)


def shards(
    inputs,
    upstream,
    master,
    moment_one,
    moment_two,
    hidden_steps,
    key_weight,
    queries,
    key_cache,
    value_cache,
    lengths,
):
    grad_factor = 1.0 / math.sqrt(inputs.shape[0] * lax.axis_size("fsdp") * lax.axis_size("tp"))
    flat = hidden_steps.reshape(16, 5120)
    weight, grad, part, fresh, attended = learn(
        inputs,
        upstream,
        master,
        moment_one,
        moment_two,
        flat,
        key_weight,
        queries,
        key_cache,
        value_cache,
        lengths,
        grad_factor,
    )
    input_grad, new_master, new_moment = finish(
        upstream, part, weight.reshape(2560, 1024), grad, master, moment_one, moment_two
    )
    fresh_kv = fresh.reshape(2, 4, 4, 128).transpose(1, 2, 0, 3)
    return (input_grad, new_master, new_moment, fresh_kv, attended)


def solution(mesh):
    in_specs = (
        P(("fsdp", "tp"), None),
        P(("fsdp", "tp"), None),
        P("fsdp", None),
        P("fsdp", None),
        P("fsdp", None),
        P(None, "fsdp", None),
        P(None, "tp"),
        P(None, "fsdp", "tp"),
        P("fsdp", None, "tp"),
        P("fsdp", None, "tp"),
        P("fsdp"),
    )
    out_specs = (
        P(("fsdp", "tp"), None),
        P("fsdp", None),
        P("fsdp", None),
        P(None, "fsdp", None, "tp"),
        P(None, "fsdp", "tp"),
    )
    return jax.shard_map(shards, mesh=mesh, in_specs=in_specs, out_specs=out_specs, check_vma=False)
```

```python
import functools
import math

import jax
import jax.numpy as jnp
from jax import lax
from jax.experimental import pallas as pl
from jax.experimental.pallas import tpu as pltpu
from jax.sharding import PartitionSpec as P

HD = 128
GROUP = 5
MESH = pl.DeviceIdType.MESH


beta_one = 0.9
beta_two = 0.95
learn_rate = 0.004
decay_rate = 0.1
adam_eps = 1e-08
correction_one = 1.0 - 0.9**20
correction_two = 1.0 - 0.95**20

T1, D1, F1, C1, A2, C2, A3, C3 = 0, 8, 16, 24, 27, 39, 42, 45
XS, UT, GX, TP, HS, FR = 48, 52, 53, 54, 62, 78
WZ, WF, WY, WS, WX, B1, B2, B3, SEMS = 94, 96, 98, 114, 122, 134, 146, 149, 152
WHOLE, QUARTER = 192, 32
NT = (((1,), (1,)), ((), ()))

f32, bf16 = jnp.float32, jnp.bfloat16


def adamw(master, grad, moment_one, moment_two):
    new_first = beta_one * moment_one + (1.0 - beta_one) * grad
    new_second = beta_two * moment_two + (1.0 - beta_two) * grad * grad
    update = new_first / correction_one / (jnp.sqrt(new_second / correction_two) + adam_eps)
    return (master - learn_rate * (update + decay_rate * master), new_first)


def learn_kernel(
    grad_factor,
    x_hbm,
    u,
    master_hbm,
    m1_hbm,
    m2_hbm,
    hidden_steps,
    kw_hbm,
    queries,
    k_hbm,
    v_hbm,
    lengths,
    wother,
    gall,
    part_hbm,
    fresh_out,
    attended,
    hidden_wide,
    hidden,
    ut,
    wsame,
    kw,
    keys,
    values,
    qf,
    acc,
    fprob,
    x_own,
    x_sib,
    ut_sib,
    master,
    m1,
    m2,
    ga,
    gb,
    gc,
    t1,
    r1a,
    r1b,
    r1c,
    s1a,
    s1b,
    s1c,
    r2a,
    r2b,
    r2c,
    s2a,
    s2b,
    s2c,
    r3a,
    r3b,
    r3c,
    gx,
    gt,
    gown,
    wpad,
    hr,
    pf,
    fr,
    ssem,
    rsem,
    lsem,
):
    f, t = lax.axis_index("fsdp"), lax.axis_index("tp")
    z, yl, c = f // 4, (f // 2) % 2, f % 2
    yh, x = t // 4, t % 4
    y = yh * 2 + yl
    sib = (z * 4 + yl * 2 + (1 - c), t)

    def dev_x(d):
        return (f, yh * 4 + (x + d) % 4)

    def dev_y(d):
        yy = (y + d) % 4
        return (z * 4 + (yy % 2) * 2 + c, (yy // 2) * 4 + x)

    def dev_z(d):
        return (((z + d) % 4) * 4 + yl * 2 + c, t)

    def rcopy(src, dst, n, who):
        return pltpu.make_async_remote_copy(
            src_ref=src,
            dst_ref=dst,
            send_sem=ssem.at[n],
            recv_sem=rsem.at[n],
            device_id=who,
            device_id_type=MESH,
        )

    def lanes(zz):
        return pl.ds(pl.multiple_of(zz * 1280, 1280), 1280)

    tcols = pl.ds(pl.multiple_of(t * 128, 128), 128)
    local = [(master_hbm, master)]
    local += [(x_hbm.at[:, lanes((z + k) % 4)], x_own.at[:, lanes((z + k) % 4)]) for k in (1, 2, 3, 4)]
    local += [(kw_hbm, kw), (k_hbm, keys), (v_hbm, values)]
    local += [(m1_hbm.at[:, tcols], m1), (m2_hbm.at[:, tcols], m2)]
    local = [pltpu.make_async_copy(a, b, lsem.at[i]) for i, (a, b) in enumerate(local)]
    for cp in local[:5]:
        cp.start()
    grad_out = pltpu.make_async_copy(gown, gall.at[t], lsem.at[10])

    barrier = pltpu.get_barrier_semaphore()

    @pl.loop(1, 16)
    def _(j):
        pl.semaphore_signal(barrier, 1, device_id=((f + j) % 16, t), device_id_type=MESH)

    @pl.loop(1, 8)
    def _(j):
        pl.semaphore_signal(barrier, 1, device_id=(f, (t + j) % 8), device_id_type=MESH)

    pl.semaphore_signal(
        barrier,
        1,
        device_id=(z * 4 + (1 - yl) * 2 + c, (1 - yh) * 4 + x),
        device_id_type=MESH,
    )

    for step in range(4):
        hidden_wide[step * 4 : (step + 1) * 4] = hidden_steps[step].astype(f32)
    hidden[...] = hidden_wide[...].astype(bf16)

    for tt in range(8):
        block = u[:, tt * 128 : (tt + 1) * 128].T
        place = ((tt % 4) * 2 + tt // 4) * 64
        ut[0, place : place + 64] = block[0:64]
        ut[1, place : place + 64] = block[64:128]
    local[0].wait()
    wsame[z, c] = master[...].astype(bf16)
    pl.semaphore_wait(barrier, 23)

    ut_copy = rcopy(ut.at[1 - c], ut_sib, UT, sib)
    ut_copy.start()
    sib_copies = [
        rcopy(x_hbm.at[:, lanes((z + k) % 4)], x_sib.at[:, lanes((z + k) % 4)], XS + k - 1, sib)
        for k in (1, 2, 3, 4)
    ]
    for cp in sib_copies[:2]:
        cp.start()

    quarter = WHOLE + x * QUARTER

    def wz(i):
        piece = wsame.at[z, c]
        return rcopy(piece, piece, WZ + i, dev_z(1 if i == 0 else 3))

    def wf(i):
        piece = wsame.at[(z + (3 if i == 0 else 1)) % 4, c, pl.ds(i * 160, 160)]
        return rcopy(piece, piece, WF + i, dev_z(1 if i == 0 else 3))

    def wy(dz, way, part):
        zz = (z + dz) % 4
        first = (way * (WHOLE // 2), pl.multiple_of(quarter + way * (QUARTER // 2), 16))[part]
        rows = pl.ds(first, (WHOLE // 2, QUARTER // 2)[part])
        return rcopy(
            wsame.at[zz, c, rows],
            wother.at[zz, c, rows],
            WY + (dz * 2 + way) * 2 + part,
            dev_y(1 if way == 0 else 3),
        )

    def wx(dz, d):
        piece = wother.at[(z + dz) % 4, c, pl.ds(pl.multiple_of(quarter, 32), QUARTER)]
        return rcopy(piece, piece, WX + dz * 3 + d - 1, dev_x(d))

    def wy_start(dz):
        for way in range(2):
            for part in range(2):
                wy(dz, way, part).start()

    def spread(dz):
        for way in range(2):
            for part in range(2):
                wy(dz, way, part).wait()
        for d in (2, 1, 3):
            wx(dz, d).start()

    def arrived(dz):
        for d in (1, 2, 3):
            wx(dz, d).wait()
        ws(dz, 1).start()

    def ws(dz, other):
        piece = (wother if other else wsame).at[(z + dz) % 4, c]
        return rcopy(piece, piece, WS + other * 4 + dz, sib)

    def part_out(dz):
        zz = (z + dz) % 4
        cols = pl.ds(pl.multiple_of(zz * 640, 640), 640)
        return pltpu.make_async_copy(x_own.at[:, cols], part_hbm.at[zz], lsem.at[11 + dz])

    def input_grad(dz):
        ws(dz, 0).wait()

        @pl.loop(0, 2)
        def _(half):
            zz = (z + dz) % 4
            cols = pl.ds(pl.multiple_of(zz * 640, 640), 640)
            rows = pl.ds(pl.multiple_of(half * 256, 256), 256)
            x_own[rows, cols] = lax.dot_general(
                u[rows], wsame[zz].reshape(640, 1024), NT, preferred_element_type=f32
            ).astype(bf16)

        part_out(dz).start()

    for i in range(2):
        wz(i).start()
    wy_start(0)

    def hidden_copy(j):
        to = (f + j) % 16
        cols = pl.ds(pl.multiple_of((to // 2) * 640, 640), 640)
        return rcopy(hidden.at[:, cols], hr.at[j], HS + j, (to, t))

    @pl.loop(1, 16)
    def _(j):
        hidden_copy(j).start()

    hr[0] = hidden[:, pl.ds(pl.multiple_of((f // 2) * 640, 640), 640)]
    wpad[...] = jnp.zeros_like(wpad)

    right, left = (x + 1) % 4, (x + 3) % 4

    def two_hop(i, zz, k):
        return rcopy(
            ga.at[(x + 2) % 4, i, zz], t1.at[i, zz], T1 + i * 4 + k, dev_x(1 if i == 0 else 3)
        )

    def direct(i, zz, k):
        piece = ga.at[right if i == 0 else left, 1 - i, zz]
        return rcopy(piece, r1a.at[i, 1 - i, zz], D1 + i * 4 + k, dev_x(1 if i == 0 else 3))

    def summed(i, zz, k):
        piece = ga.at[right if i == 0 else left, i, zz]
        return rcopy(piece, r1a.at[i, i, zz], F1 + i * 4 + k, dev_x(1 if i == 0 else 3))

    def b1(d, zz, k):
        yy = (y + d) % 4
        return rcopy(
            gb.at[:, yy // 2, zz, yy % 2], r1b.at[d - 1, :, zz], B1 + (d - 1) * 4 + k, dev_y(d)
        )

    def b2(d):
        return rcopy(s1b.at[:, (z + d) % 4], r2b.at[d - 1], B2 + d - 1, dev_z(d))

    def b3(d):
        return rcopy(s2b.at[(x + d) % 4], r3b.at[d - 1], B3 + d - 1, dev_x(d))

    def c1(d):
        return rcopy(gc.at[:, :, (z + d) % 4], r1c.at[d - 1], C1 + d - 1, dev_z(d))

    def a2(d, zz, k):
        yy = (y + d) % 4
        return rcopy(
            s1a.at[yy // 2, zz, yy % 2], r2a.at[d - 1, zz], A2 + (d - 1) * 4 + k, dev_y(d)
        )

    def c2(d):
        return rcopy(s1c.at[(x + d) % 4], r2c.at[d - 1], C2 + d - 1, dev_x(d))

    def a3(d):
        return rcopy(s2a.at[(z + d) % 4], r3a.at[d - 1], A3 + d - 1, dev_z(d))

    def c3(d):
        yy = (y + d) % 4
        return rcopy(s2c.at[yy // 2, yy % 2], r3c.at[d - 1], C3 + d - 1, dev_y(d))

    def pass_on(k):
        zz = (z + 1 + k) % 4
        for i in range(2):
            two_hop(i, zz, k).wait()
            to = right if i == 0 else left

            @pl.loop(0, 2)
            def _(ll):
                got = ga[to, i, zz, ll].astype(f32) + t1[i, zz, ll].astype(f32)
                ga[to, i, zz, ll] = got.astype(bf16)

            summed(i, zz, k).start()

    ut_copy.wait()
    for k in range(4):
        zz = (z + 1 + k) % 4
        local[1 + k].wait()
        sib_copies[k].wait()
        if k < 2:
            sib_copies[k + 2].start()

        @pl.loop(0, 4)
        def _(i):
            ll, half = i // 2, i % 2
            cols = pl.ds(pl.multiple_of(zz * 1280 + ll * 640, 640), 640)
            rows = pl.ds(pl.multiple_of(half * 256, 256), 256)
            part = jnp.dot(ut[c, rows], x_own[:, cols], preferred_element_type=f32)
            part += jnp.dot(ut_sib[rows], x_sib[:, cols], preferred_element_type=f32)
            part = part.astype(bf16)
            for b in range(4):
                xx, hh = half * 2 + b // 2, b % 2
                ga[xx, hh, zz, ll] = part[b * 64 : (b + 1) * 64, 0:384]
                gb[xx, hh, zz, ll] = part[b * 64 : (b + 1) * 64, 384:512]
                gc[xx, hh, zz, ll] = part[b * 64 : (b + 1) * 64, 512:640]

        for i in range(2):
            two_hop(i, zz, k).start()
        for i in range(2):
            direct(i, zz, k).start()
        for d in (2, 1, 3):
            b1(d, zz, k).start()
        if k < 3:
            c1(k + 1).start()
        if k > 0:
            pass_on(k - 1)
        if k == 1:
            for cp in local[5:]:
                cp.start()
            ws(0, 0).start()
    pass_on(3)

    for i in range(2):
        wz(i).wait()
    for i in range(2):
        wf(i).start()
    for dz in (1, 3):
        wy_start(dz)
        ws(dz, 0).start()

    local[5].wait()
    fresh_out[0] = jnp.dot(hidden[...], kw[...], preferred_element_type=f32).astype(bf16)
    qf[...] = jnp.zeros_like(qf)
    for step in range(4):
        for g in range(GROUP):
            qf[:, step * GROUP + g] = queries[step, :, g * HD : (g + 1) * HD].astype(f32)
    local[6].wait()
    local[7].wait()
    scale = 1.0 / math.sqrt(HD)

    def attend(r):
        q = qf[r].astype(bf16)
        scores = lax.dot_general(q, keys[r], NT, preferred_element_type=f32) * scale
        slots = lax.broadcasted_iota(jnp.int32, (32, 4096), 1)
        scores = jnp.where(slots < lengths[r], scores, -1e30)
        extra = lax.dot_general(q, fresh_out[0], NT, preferred_element_type=f32) * scale
        line = lax.broadcasted_iota(jnp.int32, (32, 16), 0)
        item = lax.broadcasted_iota(jnp.int32, (32, 16), 1)
        seen = ((item & 3) == r) & ((item >> 2) * GROUP <= line)
        extra = jnp.where(seen, extra, -1e30)
        highest = jnp.maximum(
            jnp.max(scores, axis=1, keepdims=True), jnp.max(extra, axis=1, keepdims=True)
        )
        scores = jnp.exp(scores - highest)
        extra = jnp.exp(extra - highest)
        norm = 1.0 / (
            jnp.sum(scores, axis=1, keepdims=True) + jnp.sum(extra, axis=1, keepdims=True)
        )
        fprob[r] = (extra * norm).astype(bf16)
        acc[r] = jnp.dot((scores * norm).astype(bf16), values[r], preferred_element_type=f32)

    def total(own, others, index, count=3):
        got = own.astype(f32)
        for d in range(count):
            got += others[(d,) + index].astype(f32)
        return got

    def first(k):
        zz = (z + 1 + k) % 4
        for i in range(2):
            direct(i, zz, k).wait()
            summed(i, zz, k).wait()

        @pl.loop(0, 4)
        def _(i):
            hh, ll = i // 2, i % 2
            s1a[hh, zz, ll] = total(ga[x, hh, zz, ll], r1a, (hh, zz, ll), 2).astype(bf16)

        for d in (2, 1, 3):
            a2(d, zz, k).start()

    def second(k):
        zz = (z + 1 + k) % 4
        for d in (1, 2, 3):
            a2(d, zz, k).wait()
        s2a[zz] = total(s1a[yh, zz, yl], r2a, (zz,))
        if k < 3:
            a3(k + 1).start()

    def first_b(k):
        zz = (z + 1 + k) % 4
        for d in (1, 2, 3):
            b1(d, zz, k).wait()

        @pl.loop(0, 4)
        def _(i):
            s1b[i, zz] = total(gb[i, yh, zz, yl], r1b, (i, zz)).astype(bf16)

        if k < 3:
            b2(k + 1).start()

    def second_b():
        for d in (1, 2, 3):
            b2(d).wait()

        @pl.loop(0, 4)
        def _(i):
            s2b[i] = total(s1b[i, z], r2b, (i,))

        for d in (2, 1, 3):
            b3(d).start()

    def first_c():
        for d in (1, 2, 3):
            c1(d).wait()

        @pl.loop(0, 16)
        def _(i):
            xx, hh, ll = i // 4, (i // 2) % 2, i % 2
            s1c[xx, hh, ll] = total(gc[xx, hh, z, ll], r1c, (xx, hh, ll)).astype(bf16)

        for d in (2, 1, 3):
            c2(d).start()

    def second_c():
        for d in (1, 2, 3):
            c2(d).wait()

        @pl.loop(0, 4)
        def _(i):
            hh, ll = i // 2, i % 2
            s2c[hh, ll] = total(s1c[x, hh, ll], r2c, (hh, ll))

        for d in (2, 1, 3):
            c3(d).start()

    first(0)
    first_b(0)
    pl.loop(0, 1)(attend)
    first(1)
    first_b(1)
    pl.loop(1, 2)(attend)
    spread(0)
    input_grad(0)
    first(2)
    first_b(2)
    first_c()
    second(0)
    pl.loop(2, 3)(attend)
    for i in range(2):
        wf(i).wait()
    wy_start(2)
    ws(2, 0).start()
    pl.loop(3, 4)(attend)
    first(3)
    first_b(3)
    input_grad(1)
    second(1)
    second_c()
    second_b()
    spread(1)
    spread(3)
    second(2)
    second(3)
    input_grad(3)

    for d in (1, 2, 3):
        a3(d).wait()
        b3(d).wait()
        c3(d).wait()
    gx[c, :, 0:384] = total(s2a[z], r3a, ()) * grad_factor
    gx[c, :, 384:512] = total(s2b[x], r3b, ()) * grad_factor
    gx[c, :, 512:640] = total(s2c[yh, yl], r3c, ()) * grad_factor
    gx_copy = rcopy(gx.at[c], gx.at[c], GX, sib)
    gx_copy.start()
    gx_copy.wait()
    gt[...] = gx[...].reshape(128, 640).T
    mine = pl.ds(pl.multiple_of(c * 320, 320), 320)
    gown[...] = gt[mine, :].astype(bf16)
    grad_out.start()

    def tp_copy(j):
        return rcopy(gown, gall.at[t], TP + j, (f, (t + j) % 8))

    @pl.loop(1, 8)
    def _(j):
        tp_copy(j).start()

    local[8].wait()
    local[9].wait()
    stepped, _ = adamw(master[:, tcols], gown[...].astype(f32), m1[...], m2[...])
    wpad[mine, :] = stepped.astype(bf16)

    @pl.loop(1, 16)
    def _(j):
        hidden_copy(j).wait()

    pf[...] = jnp.dot(
        hr[...].reshape(256, 640), wpad[...], preferred_element_type=f32
    ).reshape(16, 16, 128)

    def fresh_copy(j):
        return rcopy(pf.at[j], fr.at[j], FR + j, ((f + 16 - j) % 16, t))

    @pl.loop(1, 16)
    def _(j):
        fresh_copy(j).start()

    spread(2)
    for dz in (0, 1, 3):
        arrived(dz)
    input_grad(2)
    arrived(2)

    @pl.loop(1, 16)
    def _(j):
        fresh_copy(j).wait()

    fr[0] = pf[0]
    fresh_out[1] = jnp.sum(fr[...], axis=0).astype(bf16)

    @pl.loop(0, 4)
    def _(r):
        acc[r] += jnp.dot(fprob[r], fresh_out[1], preferred_element_type=f32)

    for step in range(4):
        for g in range(GROUP):
            attended[step, :, g * HD : (g + 1) * HD] = acc[:, step * GROUP + g].astype(bf16)

    grad_out.wait()

    @pl.loop(1, 8)
    def _(j):
        tp_copy(j).wait()

    for dz in range(4):
        ws(dz, 1).wait()
        part_out(dz).wait()


def learn(
    inputs, upstream, master, m1, m2, flat, key_weight, queries, keys, values, lengths, grad_factor
):
    hbm = pl.BlockSpec(memory_space=pl.ANY)
    vmem = pl.BlockSpec(memory_space=pltpu.VMEM)
    smem = pl.BlockSpec(memory_space=pltpu.SMEM)
    shape = jax.ShapeDtypeStruct
    V = pltpu.VMEM
    scratch = [
        V((16, 5120), f32),
        V((16, 5120), bf16),
        V((2, 512, 512), bf16),
        V((4, 2, 320, 1024), bf16),
        V((5120, 128), bf16),
        V((4, 4096, 128), bf16),
        V((4, 4096, 128), bf16),
        V((4, 32, 128), f32),
        V((4, 32, 128), f32),
        V((4, 32, 16), bf16),
        V((512, 5120), bf16),
        V((512, 5120), bf16),
        V((512, 512), bf16),
        V((320, 1024), f32),
        V((320, 128), f32),
        V((320, 128), f32),
        V((4, 2, 4, 2, 64, 384), bf16),
        V((4, 2, 4, 2, 64, 128), bf16),
        V((4, 2, 4, 2, 64, 128), bf16),
        V((2, 4, 2, 64, 384), bf16),
        V((2, 2, 4, 2, 64, 384), bf16),
        V((3, 4, 4, 64, 128), bf16),
        V((3, 4, 2, 2, 64, 128), bf16),
        V((2, 4, 2, 64, 384), bf16),
        V((4, 4, 64, 128), bf16),
        V((4, 2, 2, 64, 128), bf16),
        V((3, 4, 64, 384), bf16),
        V((3, 4, 64, 128), bf16),
        V((3, 2, 2, 64, 128), bf16),
        V((4, 64, 384), f32),
        V((4, 64, 128), f32),
        V((2, 2, 64, 128), f32),
        V((3, 64, 384), f32),
        V((3, 64, 128), f32),
        V((3, 64, 128), f32),
        V((2, 64, 640), f32),
        V((640, 128), f32),
        V((320, 128), bf16),
        V((640, 128), bf16),
        V((16, 16, 640), bf16),
        V((16, 16, 128), f32),
        V((16, 16, 128), f32),
        pltpu.SemaphoreType.DMA((SEMS,)),
        pltpu.SemaphoreType.DMA((SEMS,)),
        pltpu.SemaphoreType.DMA((15,)),
    ]
    return pl.pallas_call(
        functools.partial(learn_kernel, grad_factor),
        out_shape=(
            shape((4, 2, 320, 1024), bf16),
            shape((8, 320, 128), bf16),
            shape((4, 512, 640), bf16),
            shape((2, 16, 128), bf16),
            shape((4, 4, 640), bf16),
        ),
        in_specs=[hbm, vmem, hbm, hbm, hbm, vmem, hbm, vmem, hbm, hbm, smem],
        out_specs=[hbm, hbm, hbm, vmem, vmem],
        scratch_shapes=scratch,
        name="learn",
        compiler_params=pltpu.CompilerParams(
            collective_id=0, has_side_effects=True, vmem_limit_bytes=56 << 20
        ),
    )(inputs, upstream, master, m1, m2, flat, key_weight, queries, keys, values, lengths)


def finish_kernel(
    u, part, w, grad, master, m1, m2, fresh, heads, input_grad, new_master, new_moment, kv, attended
):
    @pl.when(pl.program_id(0) == 0)
    def _():
        wide = fresh[...].astype(f32).reshape(2, 4, 4, 128)
        kv[...] = jnp.stack([wide[0], wide[1]], axis=2).astype(bf16)
        attended[...] = heads[...]

    yl = (lax.axis_index("fsdp") // 2) % 2
    same = pl.ds(pl.multiple_of(yl * 640, 640), 640)
    other = pl.ds(pl.multiple_of((1 - yl) * 640, 640), 640)
    input_grad[:, same] = part[...]
    input_grad[:, other] = lax.dot_general(
        u[...], w[...], NT, preferred_element_type=f32
    ).astype(bf16)
    for i in range(2):
        cols = slice(i * 128, (i + 1) * 128)
        new_master[:, cols], new_moment[:, cols] = adamw(
            master[:, cols], grad[i].astype(f32), m1[:, cols], m2[:, cols]
        )


def finish(upstream, part, weight, grad, master, m1, m2, fresh, heads):
    vmem = pl.BlockSpec(memory_space=pltpu.VMEM)
    cols = pl.BlockSpec((320, 256), lambda i: (0, i))
    return pl.pallas_call(
        finish_kernel,
        grid=(4,),
        out_shape=(
            jax.ShapeDtypeStruct((512, 5120), bf16),
            jax.ShapeDtypeStruct((320, 1024), f32),
            jax.ShapeDtypeStruct((320, 1024), f32),
            jax.ShapeDtypeStruct((4, 4, 2, 128), bf16),
            jax.ShapeDtypeStruct((4, 4, 640), bf16),
        ),
        in_specs=[
            pl.BlockSpec((512, 1024), lambda i: (0, 0)),
            pl.BlockSpec((None, 512, 640), lambda i: (i, 0, 0)),
            pl.BlockSpec((640, 1024), lambda i: (i, 0)),
            pl.BlockSpec((2, 320, 128), lambda i: (i, 0, 0)),
            cols,
            cols,
            cols,
            vmem,
            vmem,
        ],
        out_specs=[pl.BlockSpec((512, 1280), lambda i: (0, i)), cols, cols, vmem, vmem],
        name="finish",
        compiler_params=pltpu.CompilerParams(vmem_limit_bytes=60 << 20),
    )(upstream, part, weight, grad, master, m1, m2, fresh, heads)


def shards(
    inputs,
    upstream,
    master,
    moment_one,
    moment_two,
    hidden_steps,
    key_weight,
    queries,
    key_cache,
    value_cache,
    lengths,
):
    grad_factor = 1.0 / math.sqrt(inputs.shape[0] * lax.axis_size("fsdp") * lax.axis_size("tp"))
    weight, grad, part, fresh, attended = learn(
        inputs,
        upstream,
        master,
        moment_one,
        moment_two,
        hidden_steps,
        key_weight,
        queries,
        key_cache,
        value_cache,
        lengths,
        grad_factor,
    )
    return finish(
        upstream,
        part,
        weight.reshape(2560, 1024),
        grad,
        master,
        moment_one,
        moment_two,
        fresh,
        attended,
    )


def solution(mesh):
    in_specs = (
        P(("fsdp", "tp"), None),
        P(("fsdp", "tp"), None),
        P("fsdp", None),
        P("fsdp", None),
        P("fsdp", None),
        P(None, "fsdp", None),
        P(None, "tp"),
        P(None, "fsdp", "tp"),
        P("fsdp", None, "tp"),
        P("fsdp", None, "tp"),
        P("fsdp"),
    )
    out_specs = (
        P(("fsdp", "tp"), None),
        P("fsdp", None),
        P("fsdp", None),
        P(None, "fsdp", None, "tp"),
        P(None, "fsdp", "tp"),
    )
    return jax.shard_map(shards, mesh=mesh, in_specs=in_specs, out_specs=out_specs, check_vma=False)
```

```python
import functools
import math

import jax
import jax.numpy as jnp
from jax import lax
from jax.experimental import pallas as pl
from jax.experimental.pallas import tpu as pltpu
from jax.sharding import PartitionSpec as P

HD = 128
GROUP = 5
MESH = pl.DeviceIdType.MESH


beta_one = 0.9
beta_two = 0.95
learn_rate = 0.004
decay_rate = 0.1
adam_eps = 1e-08
correction_one = 1.0 - 0.9**20
correction_two = 1.0 - 0.95**20

T1, D1, F1, C1, A2, C2, A3, C3 = 0, 8, 16, 24, 27, 39, 42, 45
XS, UT, GX, TP, HS, FR = 48, 52, 53, 54, 62, 78
WZ, WF, WY, WS, WX, B1, B2, B3, SEMS = 94, 96, 98, 114, 122, 134, 146, 149, 152
WHOLE, QUARTER = 192, 32
NT = (((1,), (1,)), ((), ()))

f32, bf16 = jnp.float32, jnp.bfloat16


def adamw(master, grad, moment_one, moment_two):
    new_first = beta_one * moment_one + (1.0 - beta_one) * grad
    new_second = beta_two * moment_two + (1.0 - beta_two) * grad * grad
    update = new_first / correction_one / (jnp.sqrt(new_second / correction_two) + adam_eps)
    return (master - learn_rate * (update + decay_rate * master), new_first)


def learn_kernel(
    grad_factor,
    x_hbm,
    u,
    master_hbm,
    m1_hbm,
    m2_hbm,
    hidden_steps,
    kw_hbm,
    queries,
    k_hbm,
    v_hbm,
    lengths,
    wother,
    gall,
    part_hbm,
    fresh_out,
    attended,
    hidden_wide,
    hidden,
    ut,
    wsame,
    kw,
    keys,
    values,
    qf,
    acc,
    fprob,
    x_own,
    x_sib,
    ut_sib,
    master,
    m1,
    m2,
    ga,
    gb,
    gc,
    t1,
    r1a,
    r1b,
    r1c,
    s1a,
    s1b,
    s1c,
    r2a,
    r2b,
    r2c,
    s2a,
    s2b,
    s2c,
    r3a,
    r3b,
    r3c,
    gx,
    gt,
    gown,
    wpad,
    hr,
    pf,
    fr,
    ssem,
    rsem,
    lsem,
):
    f, t = lax.axis_index("fsdp"), lax.axis_index("tp")
    z, yl, c = f // 4, (f // 2) % 2, f % 2
    yh, x = t // 4, t % 4
    y = yh * 2 + yl
    sib = (z * 4 + yl * 2 + (1 - c), t)

    def dev_x(d):
        return (f, yh * 4 + (x + d) % 4)

    def dev_y(d):
        yy = (y + d) % 4
        return (z * 4 + (yy % 2) * 2 + c, (yy // 2) * 4 + x)

    def dev_z(d):
        return (((z + d) % 4) * 4 + yl * 2 + c, t)

    def rcopy(src, dst, n, who):
        return pltpu.make_async_remote_copy(
            src_ref=src,
            dst_ref=dst,
            send_sem=ssem.at[n],
            recv_sem=rsem.at[n],
            device_id=who,
            device_id_type=MESH,
        )

    def lanes(zz):
        return pl.ds(pl.multiple_of(zz * 1280, 1280), 1280)

    tcols = pl.ds(pl.multiple_of(t * 128, 128), 128)
    local = [(master_hbm, master)]
    local += [(x_hbm.at[:, lanes((z + k) % 4)], x_own.at[:, lanes((z + k) % 4)]) for k in (1, 2, 3, 4)]
    local += [(kw_hbm, kw), (k_hbm, keys), (v_hbm, values)]
    local += [(m1_hbm.at[:, tcols], m1), (m2_hbm.at[:, tcols], m2)]
    local = [pltpu.make_async_copy(a, b, lsem.at[i]) for i, (a, b) in enumerate(local)]
    for cp in local[:5]:
        cp.start()
    grad_out = pltpu.make_async_copy(gown, gall.at[t], lsem.at[10])

    barrier = pltpu.get_barrier_semaphore()

    @pl.loop(1, 16)
    def _(j):
        pl.semaphore_signal(barrier, 1, device_id=((f + j) % 16, t), device_id_type=MESH)

    @pl.loop(1, 8)
    def _(j):
        pl.semaphore_signal(barrier, 1, device_id=(f, (t + j) % 8), device_id_type=MESH)

    pl.semaphore_signal(
        barrier,
        1,
        device_id=(z * 4 + (1 - yl) * 2 + c, (1 - yh) * 4 + x),
        device_id_type=MESH,
    )

    for step in range(4):
        hidden_wide[step * 4 : (step + 1) * 4] = hidden_steps[step].astype(f32)
    hidden[...] = hidden_wide[...].astype(bf16)

    for tt in range(8):
        block = u[:, tt * 128 : (tt + 1) * 128].T
        place = ((tt % 4) * 2 + tt // 4) * 64
        ut[0, place : place + 64] = block[0:64]
        ut[1, place : place + 64] = block[64:128]
    local[0].wait()
    wsame[z, c] = master[...].astype(bf16)
    pl.semaphore_wait(barrier, 23)

    ut_copy = rcopy(ut.at[1 - c], ut_sib, UT, sib)
    ut_copy.start()
    sib_copies = [
        rcopy(x_hbm.at[:, lanes((z + k) % 4)], x_sib.at[:, lanes((z + k) % 4)], XS + k - 1, sib)
        for k in (1, 2, 3, 4)
    ]
    for cp in sib_copies[:2]:
        cp.start()

    quarter = WHOLE + x * QUARTER

    def wz(i):
        piece = wsame.at[z, c]
        return rcopy(piece, piece, WZ + i, dev_z(1 if i == 0 else 3))

    def wf(i):
        piece = wsame.at[(z + (3 if i == 0 else 1)) % 4, c, pl.ds(i * 160, 160)]
        return rcopy(piece, piece, WF + i, dev_z(1 if i == 0 else 3))

    def wy(dz, way, part):
        zz = (z + dz) % 4
        first = (way * (WHOLE // 2), pl.multiple_of(quarter + way * (QUARTER // 2), 16))[part]
        rows = pl.ds(first, (WHOLE // 2, QUARTER // 2)[part])
        return rcopy(
            wsame.at[zz, c, rows],
            wother.at[zz, c, rows],
            WY + (dz * 2 + way) * 2 + part,
            dev_y(1 if way == 0 else 3),
        )

    def wx(dz, d):
        piece = wother.at[(z + dz) % 4, c, pl.ds(pl.multiple_of(quarter, 32), QUARTER)]
        return rcopy(piece, piece, WX + dz * 3 + d - 1, dev_x(d))

    def wy_start(dz):
        for way in range(2):
            for part in range(2):
                wy(dz, way, part).start()

    def spread(dz):
        for way in range(2):
            for part in range(2):
                wy(dz, way, part).wait()
        for d in (2, 1, 3):
            wx(dz, d).start()

    def arrived(dz):
        for d in (1, 2, 3):
            wx(dz, d).wait()
        ws(dz, 1).start()

    def ws(dz, other):
        piece = (wother if other else wsame).at[(z + dz) % 4, c]
        return rcopy(piece, piece, WS + other * 4 + dz, sib)

    def part_out(dz):
        zz = (z + dz) % 4
        cols = pl.ds(pl.multiple_of(zz * 640, 640), 640)
        return pltpu.make_async_copy(x_own.at[:, cols], part_hbm.at[zz], lsem.at[11 + dz])

    def input_grad(dz):
        ws(dz, 0).wait()

        @pl.loop(0, 2)
        def _(half):
            zz = (z + dz) % 4
            cols = pl.ds(pl.multiple_of(zz * 640, 640), 640)
            rows = pl.ds(pl.multiple_of(half * 256, 256), 256)
            x_own[rows, cols] = lax.dot_general(
                u[rows], wsame[zz].reshape(640, 1024), NT, preferred_element_type=f32
            ).astype(bf16)

        part_out(dz).start()

    for i in range(2):
        wz(i).start()
    wy_start(0)

    def hidden_copy(j):
        to = (f + j) % 16
        cols = pl.ds(pl.multiple_of((to // 2) * 640, 640), 640)
        return rcopy(hidden.at[:, cols], hr.at[j], HS + j, (to, t))

    @pl.loop(1, 16)
    def _(j):
        hidden_copy(j).start()

    hr[0] = hidden[:, pl.ds(pl.multiple_of((f // 2) * 640, 640), 640)]
    wpad[...] = jnp.zeros_like(wpad)

    right, left = (x + 1) % 4, (x + 3) % 4

    def two_hop(i, zz, k):
        return rcopy(
            ga.at[(x + 2) % 4, i, zz], t1.at[i, zz], T1 + i * 4 + k, dev_x(1 if i == 0 else 3)
        )

    def direct(i, zz, k):
        piece = ga.at[right if i == 0 else left, 1 - i, zz]
        return rcopy(piece, r1a.at[i, 1 - i, zz], D1 + i * 4 + k, dev_x(1 if i == 0 else 3))

    def summed(i, zz, k):
        piece = ga.at[right if i == 0 else left, i, zz]
        return rcopy(piece, r1a.at[i, i, zz], F1 + i * 4 + k, dev_x(1 if i == 0 else 3))

    def b1(d, zz, k):
        yy = (y + d) % 4
        return rcopy(
            gb.at[:, yy // 2, zz, yy % 2], r1b.at[d - 1, :, zz], B1 + (d - 1) * 4 + k, dev_y(d)
        )

    def b2(d):
        return rcopy(s1b.at[:, (z + d) % 4], r2b.at[d - 1], B2 + d - 1, dev_z(d))

    def b3(d):
        return rcopy(s2b.at[(x + d) % 4], r3b.at[d - 1], B3 + d - 1, dev_x(d))

    def c1(d):
        return rcopy(gc.at[:, :, (z + d) % 4], r1c.at[d - 1], C1 + d - 1, dev_z(d))

    def a2(d, zz, k):
        yy = (y + d) % 4
        return rcopy(
            s1a.at[yy // 2, zz, yy % 2], r2a.at[d - 1, zz], A2 + (d - 1) * 4 + k, dev_y(d)
        )

    def c2(d):
        return rcopy(s1c.at[(x + d) % 4], r2c.at[d - 1], C2 + d - 1, dev_x(d))

    def a3(d):
        return rcopy(s2a.at[(z + d) % 4], r3a.at[d - 1], A3 + d - 1, dev_z(d))

    def c3(d):
        yy = (y + d) % 4
        return rcopy(s2c.at[yy // 2, yy % 2], r3c.at[d - 1], C3 + d - 1, dev_y(d))

    def pass_on(k):
        zz = (z + 1 + k) % 4
        for i in range(2):
            two_hop(i, zz, k).wait()
            to = right if i == 0 else left

            @pl.loop(0, 2)
            def _(ll):
                got = ga[to, i, zz, ll].astype(f32) + t1[i, zz, ll].astype(f32)
                ga[to, i, zz, ll] = got.astype(bf16)

            summed(i, zz, k).start()

    ut_copy.wait()
    for k in range(4):
        zz = (z + 1 + k) % 4
        local[1 + k].wait()
        sib_copies[k].wait()
        if k < 2:
            sib_copies[k + 2].start()

        @pl.loop(0, 4)
        def _(i):
            ll, half = i // 2, i % 2
            cols = pl.ds(pl.multiple_of(zz * 1280 + ll * 640, 640), 640)
            rows = pl.ds(pl.multiple_of(half * 256, 256), 256)
            part = jnp.dot(ut[c, rows], x_own[:, cols], preferred_element_type=f32)
            part += jnp.dot(ut_sib[rows], x_sib[:, cols], preferred_element_type=f32)
            part = part.astype(bf16)
            for b in range(4):
                xx, hh = half * 2 + b // 2, b % 2
                ga[xx, hh, zz, ll] = part[b * 64 : (b + 1) * 64, 0:384]
                gb[xx, hh, zz, ll] = part[b * 64 : (b + 1) * 64, 384:512]
                gc[xx, hh, zz, ll] = part[b * 64 : (b + 1) * 64, 512:640]

        for i in range(2):
            two_hop(i, zz, k).start()
        for i in range(2):
            direct(i, zz, k).start()
        for d in (2, 1, 3):
            b1(d, zz, k).start()
        if k < 3:
            c1(k + 1).start()
        if k > 0:
            pass_on(k - 1)
        if k == 1:
            for cp in local[5:]:
                cp.start()
            ws(0, 0).start()

    for i in range(2):
        wz(i).wait()
    for i in range(2):
        wf(i).start()
    for dz in (1, 3):
        wy_start(dz)
        ws(dz, 0).start()
    pass_on(3)


    local[5].wait()
    fresh_out[0] = jnp.dot(hidden[...], kw[...], preferred_element_type=f32).astype(bf16)
    qf[...] = jnp.zeros_like(qf)
    for step in range(4):
        for g in range(GROUP):
            qf[:, step * GROUP + g] = queries[step, :, g * HD : (g + 1) * HD].astype(f32)
    local[6].wait()
    local[7].wait()
    scale = 1.0 / math.sqrt(HD)

    def attend(r):
        q = qf[r].astype(bf16)
        scores = lax.dot_general(q, keys[r], NT, preferred_element_type=f32) * scale
        slots = lax.broadcasted_iota(jnp.int32, (32, 4096), 1)
        scores = jnp.where(slots < lengths[r], scores, -1e30)
        extra = lax.dot_general(q, fresh_out[0], NT, preferred_element_type=f32) * scale
        line = lax.broadcasted_iota(jnp.int32, (32, 16), 0)
        item = lax.broadcasted_iota(jnp.int32, (32, 16), 1)
        seen = ((item & 3) == r) & ((item >> 2) * GROUP <= line)
        extra = jnp.where(seen, extra, -1e30)
        highest = jnp.maximum(
            jnp.max(scores, axis=1, keepdims=True), jnp.max(extra, axis=1, keepdims=True)
        )
        scores = jnp.exp(scores - highest)
        extra = jnp.exp(extra - highest)
        norm = 1.0 / (
            jnp.sum(scores, axis=1, keepdims=True) + jnp.sum(extra, axis=1, keepdims=True)
        )
        fprob[r] = (extra * norm).astype(bf16)
        acc[r] = jnp.dot((scores * norm).astype(bf16), values[r], preferred_element_type=f32)

    def total(own, others, index, count=3):
        got = own.astype(f32)
        for d in range(count):
            got += others[(d,) + index].astype(f32)
        return got

    def first(k):
        zz = (z + 1 + k) % 4
        for i in range(2):
            direct(i, zz, k).wait()
            summed(i, zz, k).wait()

        @pl.loop(0, 4)
        def _(i):
            hh, ll = i // 2, i % 2
            s1a[hh, zz, ll] = total(ga[x, hh, zz, ll], r1a, (hh, zz, ll), 2).astype(bf16)

        for d in (2, 1, 3):
            a2(d, zz, k).start()

    def second(k):
        zz = (z + 1 + k) % 4
        for d in (1, 2, 3):
            a2(d, zz, k).wait()
        s2a[zz] = total(s1a[yh, zz, yl], r2a, (zz,))
        if k < 3:
            a3(k + 1).start()

    def first_b(k):
        zz = (z + 1 + k) % 4
        for d in (1, 2, 3):
            b1(d, zz, k).wait()

        @pl.loop(0, 4)
        def _(i):
            s1b[i, zz] = total(gb[i, yh, zz, yl], r1b, (i, zz)).astype(bf16)

        if k < 3:
            b2(k + 1).start()

    def second_b():
        for d in (1, 2, 3):
            b2(d).wait()

        @pl.loop(0, 4)
        def _(i):
            s2b[i] = total(s1b[i, z], r2b, (i,))

        for d in (2, 1, 3):
            b3(d).start()

    def first_c():
        for d in (1, 2, 3):
            c1(d).wait()

        @pl.loop(0, 16)
        def _(i):
            xx, hh, ll = i // 4, (i // 2) % 2, i % 2
            s1c[xx, hh, ll] = total(gc[xx, hh, z, ll], r1c, (xx, hh, ll)).astype(bf16)

        for d in (2, 1, 3):
            c2(d).start()

    def second_c():
        for d in (1, 2, 3):
            c2(d).wait()

        @pl.loop(0, 4)
        def _(i):
            hh, ll = i // 2, i % 2
            s2c[hh, ll] = total(s1c[x, hh, ll], r2c, (hh, ll))

        for d in (2, 1, 3):
            c3(d).start()

    first(0)
    first_b(0)
    pl.loop(0, 1)(attend)
    first(1)
    first_b(1)
    pl.loop(1, 2)(attend)
    spread(0)
    input_grad(0)
    first(2)
    first_b(2)
    first_c()
    second(0)
    pl.loop(2, 3)(attend)
    for i in range(2):
        wf(i).wait()
    wy_start(2)
    ws(2, 0).start()
    pl.loop(3, 4)(attend)
    first(3)
    first_b(3)
    input_grad(1)
    second(1)
    second_c()
    second_b()
    spread(1)
    spread(3)
    second(2)
    second(3)
    spread(2)
    input_grad(3)

    for d in (1, 2, 3):
        a3(d).wait()
        b3(d).wait()
        c3(d).wait()
    gx[c, :, 0:384] = total(s2a[z], r3a, ()) * grad_factor
    gx[c, :, 384:512] = total(s2b[x], r3b, ()) * grad_factor
    gx[c, :, 512:640] = total(s2c[yh, yl], r3c, ()) * grad_factor
    gx_copy = rcopy(gx.at[c], gx.at[c], GX, sib)
    gx_copy.start()
    gx_copy.wait()
    gt[...] = gx[...].reshape(128, 640).T
    mine = pl.ds(pl.multiple_of(c * 320, 320), 320)
    gown[...] = gt[mine, :].astype(bf16)
    grad_out.start()

    def tp_copy(j):
        return rcopy(gown, gall.at[t], TP + j, (f, (t + j) % 8))

    @pl.loop(1, 8)
    def _(j):
        tp_copy(j).start()

    local[8].wait()
    local[9].wait()
    stepped, _ = adamw(master[:, tcols], gown[...].astype(f32), m1[...], m2[...])
    wpad[mine, :] = stepped.astype(bf16)

    @pl.loop(1, 16)
    def _(j):
        hidden_copy(j).wait()

    pf[...] = jnp.dot(
        hr[...].reshape(256, 640), wpad[...], preferred_element_type=f32
    ).reshape(16, 16, 128)

    def fresh_copy(j):
        return rcopy(pf.at[j], fr.at[j], FR + j, ((f + 16 - j) % 16, t))

    @pl.loop(1, 16)
    def _(j):
        fresh_copy(j).start()

    for dz in (0, 1, 3, 2):
        arrived(dz)
    input_grad(2)

    @pl.loop(1, 16)
    def _(j):
        fresh_copy(j).wait()

    fr[0] = pf[0]
    fresh_out[1] = jnp.sum(fr[...], axis=0).astype(bf16)

    @pl.loop(0, 4)
    def _(r):
        acc[r] += jnp.dot(fprob[r], fresh_out[1], preferred_element_type=f32)

    for step in range(4):
        for g in range(GROUP):
            attended[step, :, g * HD : (g + 1) * HD] = acc[:, step * GROUP + g].astype(bf16)

    grad_out.wait()

    @pl.loop(1, 8)
    def _(j):
        tp_copy(j).wait()

    for dz in range(4):
        ws(dz, 1).wait()
        part_out(dz).wait()


def learn(
    inputs, upstream, master, m1, m2, flat, key_weight, queries, keys, values, lengths, grad_factor
):
    hbm = pl.BlockSpec(memory_space=pl.ANY)
    vmem = pl.BlockSpec(memory_space=pltpu.VMEM)
    smem = pl.BlockSpec(memory_space=pltpu.SMEM)
    shape = jax.ShapeDtypeStruct
    V = pltpu.VMEM
    scratch = [
        V((16, 5120), f32),
        V((16, 5120), bf16),
        V((2, 512, 512), bf16),
        V((4, 2, 320, 1024), bf16),
        V((5120, 128), bf16),
        V((4, 4096, 128), bf16),
        V((4, 4096, 128), bf16),
        V((4, 32, 128), f32),
        V((4, 32, 128), f32),
        V((4, 32, 16), bf16),
        V((512, 5120), bf16),
        V((512, 5120), bf16),
        V((512, 512), bf16),
        V((320, 1024), f32),
        V((320, 128), f32),
        V((320, 128), f32),
        V((4, 2, 4, 2, 64, 384), bf16),
        V((4, 2, 4, 2, 64, 128), bf16),
        V((4, 2, 4, 2, 64, 128), bf16),
        V((2, 4, 2, 64, 384), bf16),
        V((2, 2, 4, 2, 64, 384), bf16),
        V((3, 4, 4, 64, 128), bf16),
        V((3, 4, 2, 2, 64, 128), bf16),
        V((2, 4, 2, 64, 384), bf16),
        V((4, 4, 64, 128), bf16),
        V((4, 2, 2, 64, 128), bf16),
        V((3, 4, 64, 384), bf16),
        V((3, 4, 64, 128), bf16),
        V((3, 2, 2, 64, 128), bf16),
        V((4, 64, 384), f32),
        V((4, 64, 128), f32),
        V((2, 2, 64, 128), f32),
        V((3, 64, 384), f32),
        V((3, 64, 128), f32),
        V((3, 64, 128), f32),
        V((2, 64, 640), f32),
        V((640, 128), f32),
        V((320, 128), bf16),
        V((640, 128), bf16),
        V((16, 16, 640), bf16),
        V((16, 16, 128), f32),
        V((16, 16, 128), f32),
        pltpu.SemaphoreType.DMA((SEMS,)),
        pltpu.SemaphoreType.DMA((SEMS,)),
        pltpu.SemaphoreType.DMA((15,)),
    ]
    return pl.pallas_call(
        functools.partial(learn_kernel, grad_factor),
        out_shape=(
            shape((4, 2, 320, 1024), bf16),
            shape((8, 320, 128), bf16),
            shape((4, 512, 640), bf16),
            shape((2, 16, 128), bf16),
            shape((4, 4, 640), bf16),
        ),
        in_specs=[hbm, vmem, hbm, hbm, hbm, vmem, hbm, vmem, hbm, hbm, smem],
        out_specs=[hbm, hbm, hbm, vmem, vmem],
        scratch_shapes=scratch,
        name="learn",
        compiler_params=pltpu.CompilerParams(
            collective_id=0, has_side_effects=True, vmem_limit_bytes=56 << 20
        ),
    )(inputs, upstream, master, m1, m2, flat, key_weight, queries, keys, values, lengths)


def finish_kernel(
    u, part, w, grad, master, m1, m2, fresh, heads, input_grad, new_master, new_moment, kv, attended
):
    @pl.when(pl.program_id(0) == 0)
    def _():
        wide = fresh[...].astype(f32).reshape(2, 4, 4, 128)
        kv[...] = jnp.stack([wide[0], wide[1]], axis=2).astype(bf16)
        attended[...] = heads[...]

    yl = (lax.axis_index("fsdp") // 2) % 2
    same = pl.ds(pl.multiple_of(yl * 640, 640), 640)
    other = pl.ds(pl.multiple_of((1 - yl) * 640, 640), 640)
    input_grad[:, same] = part[...]
    input_grad[:, other] = lax.dot_general(
        u[...], w[...], NT, preferred_element_type=f32
    ).astype(bf16)
    for i in range(2):
        cols = slice(i * 128, (i + 1) * 128)
        new_master[:, cols], new_moment[:, cols] = adamw(
            master[:, cols], grad[i].astype(f32), m1[:, cols], m2[:, cols]
        )


def finish(upstream, part, weight, grad, master, m1, m2, fresh, heads):
    vmem = pl.BlockSpec(memory_space=pltpu.VMEM)
    cols = pl.BlockSpec((320, 256), lambda i: (0, i))
    return pl.pallas_call(
        finish_kernel,
        grid=(4,),
        out_shape=(
            jax.ShapeDtypeStruct((512, 5120), bf16),
            jax.ShapeDtypeStruct((320, 1024), f32),
            jax.ShapeDtypeStruct((320, 1024), f32),
            jax.ShapeDtypeStruct((4, 4, 2, 128), bf16),
            jax.ShapeDtypeStruct((4, 4, 640), bf16),
        ),
        in_specs=[
            pl.BlockSpec((512, 1024), lambda i: (0, 0)),
            pl.BlockSpec((None, 512, 640), lambda i: (i, 0, 0)),
            pl.BlockSpec((640, 1024), lambda i: (i, 0)),
            pl.BlockSpec((2, 320, 128), lambda i: (i, 0, 0)),
            cols,
            cols,
            cols,
            vmem,
            vmem,
        ],
        out_specs=[pl.BlockSpec((512, 1280), lambda i: (0, i)), cols, cols, vmem, vmem],
        name="finish",
        compiler_params=pltpu.CompilerParams(vmem_limit_bytes=60 << 20),
    )(upstream, part, weight, grad, master, m1, m2, fresh, heads)


def shards(
    inputs,
    upstream,
    master,
    moment_one,
    moment_two,
    hidden_steps,
    key_weight,
    queries,
    key_cache,
    value_cache,
    lengths,
):
    grad_factor = 1.0 / math.sqrt(inputs.shape[0] * lax.axis_size("fsdp") * lax.axis_size("tp"))
    weight, grad, part, fresh, attended = learn(
        inputs,
        upstream,
        master,
        moment_one,
        moment_two,
        hidden_steps,
        key_weight,
        queries,
        key_cache,
        value_cache,
        lengths,
        grad_factor,
    )
    return finish(
        upstream,
        part,
        weight.reshape(2560, 1024),
        grad,
        master,
        moment_one,
        moment_two,
        fresh,
        attended,
    )


def solution(mesh):
    in_specs = (
        P(("fsdp", "tp"), None),
        P(("fsdp", "tp"), None),
        P("fsdp", None),
        P("fsdp", None),
        P("fsdp", None),
        P(None, "fsdp", None),
        P(None, "tp"),
        P(None, "fsdp", "tp"),
        P("fsdp", None, "tp"),
        P("fsdp", None, "tp"),
        P("fsdp"),
    )
    out_specs = (
        P(("fsdp", "tp"), None),
        P("fsdp", None),
        P("fsdp", None),
        P(None, "fsdp", None, "tp"),
        P(None, "fsdp", "tp"),
    )
    return jax.shard_map(shards, mesh=mesh, in_specs=in_specs, out_specs=out_specs, check_vma=False)
```

```python
import functools
import math

import jax
import jax.numpy as jnp
from jax import lax
from jax.experimental import pallas as pl
from jax.experimental.pallas import tpu as pltpu
from jax.sharding import PartitionSpec as P

HD = 128
GROUP = 5
MESH = pl.DeviceIdType.MESH


beta_one = 0.9
beta_two = 0.95
learn_rate = 0.004
decay_rate = 0.1
adam_eps = 1e-08
correction_one = 1.0 - 0.9**20
correction_two = 1.0 - 0.95**20

T1, D1, F1, C1, A2, C2, A3, C3 = 0, 8, 16, 24, 27, 39, 42, 45
XS, UT, GX, TP, HS, FR = 48, 52, 53, 54, 62, 78
WZ, WF, WY, WS, WX, B1, B2, B3, SEMS = 94, 96, 98, 114, 122, 134, 146, 149, 152
WHOLE, QUARTER = 192, 32
NT = (((1,), (1,)), ((), ()))

f32, bf16 = jnp.float32, jnp.bfloat16


def adamw(master, grad, moment_one, moment_two):
    new_first = beta_one * moment_one + (1.0 - beta_one) * grad
    new_second = beta_two * moment_two + (1.0 - beta_two) * grad * grad
    update = new_first / correction_one / (jnp.sqrt(new_second / correction_two) + adam_eps)
    return (master - learn_rate * (update + decay_rate * master), new_first)


def learn_kernel(
    grad_factor,
    x_hbm,
    u,
    master_hbm,
    m1_hbm,
    m2_hbm,
    hidden_steps,
    kw_hbm,
    queries,
    k_hbm,
    v_hbm,
    lengths,
    wother,
    gall,
    part_hbm,
    fresh_out,
    attended,
    hidden_wide,
    hidden,
    ut,
    wsame,
    kw,
    keys,
    values,
    qf,
    acc,
    fprob,
    x_own,
    x_sib,
    ut_sib,
    master,
    m1,
    m2,
    ga,
    gb,
    gc,
    t1,
    r1a,
    r1b,
    r1c,
    s1a,
    s1b,
    s1c,
    r2a,
    r2b,
    r2c,
    s2a,
    s2b,
    s2c,
    r3a,
    r3b,
    r3c,
    gx,
    gt,
    gown,
    wpad,
    hr,
    pf,
    fr,
    ssem,
    rsem,
    lsem,
):
    f, t = lax.axis_index("fsdp"), lax.axis_index("tp")
    z, yl, c = f // 4, (f // 2) % 2, f % 2
    yh, x = t // 4, t % 4
    y = yh * 2 + yl
    sib = (z * 4 + yl * 2 + (1 - c), t)

    def dev_x(d):
        return (f, yh * 4 + (x + d) % 4)

    def dev_y(d):
        yy = (y + d) % 4
        return (z * 4 + (yy % 2) * 2 + c, (yy // 2) * 4 + x)

    def dev_z(d):
        return (((z + d) % 4) * 4 + yl * 2 + c, t)

    def rcopy(src, dst, n, who):
        return pltpu.make_async_remote_copy(
            src_ref=src,
            dst_ref=dst,
            send_sem=ssem.at[n],
            recv_sem=rsem.at[n],
            device_id=who,
            device_id_type=MESH,
        )

    def lanes(zz):
        return pl.ds(pl.multiple_of(zz * 1280, 1280), 1280)

    tcols = pl.ds(pl.multiple_of(t * 128, 128), 128)
    local = [(master_hbm, master)]
    local += [(x_hbm.at[:, lanes((z + k) % 4)], x_own.at[:, lanes((z + k) % 4)]) for k in (1, 2, 3, 4)]
    local += [(kw_hbm, kw), (k_hbm, keys), (v_hbm, values)]
    local += [(m1_hbm.at[:, tcols], m1), (m2_hbm.at[:, tcols], m2)]
    local = [pltpu.make_async_copy(a, b, lsem.at[i]) for i, (a, b) in enumerate(local)]
    for cp in local[:5]:
        cp.start()
    grad_out = pltpu.make_async_copy(gown, gall.at[t], lsem.at[10])

    barrier = pltpu.get_barrier_semaphore()

    @pl.loop(1, 16)
    def _(j):
        pl.semaphore_signal(barrier, 1, device_id=((f + j) % 16, t), device_id_type=MESH)

    @pl.loop(1, 8)
    def _(j):
        pl.semaphore_signal(barrier, 1, device_id=(f, (t + j) % 8), device_id_type=MESH)

    pl.semaphore_signal(
        barrier,
        1,
        device_id=(z * 4 + (1 - yl) * 2 + c, (1 - yh) * 4 + x),
        device_id_type=MESH,
    )

    for step in range(4):
        hidden_wide[step * 4 : (step + 1) * 4] = hidden_steps[step].astype(f32)
    hidden[...] = hidden_wide[...].astype(bf16)

    for tt in range(8):
        block = u[:, tt * 128 : (tt + 1) * 128].T
        place = ((tt % 4) * 2 + tt // 4) * 64
        ut[0, place : place + 64] = block[0:64]
        ut[1, place : place + 64] = block[64:128]
    local[0].wait()
    wsame[z, c] = master[...].astype(bf16)
    pl.semaphore_wait(barrier, 23)

    ut_copy = rcopy(ut.at[1 - c], ut_sib, UT, sib)
    ut_copy.start()
    sib_copies = [
        rcopy(x_hbm.at[:, lanes((z + k) % 4)], x_sib.at[:, lanes((z + k) % 4)], XS + k - 1, sib)
        for k in (1, 2, 3, 4)
    ]
    for cp in sib_copies[:2]:
        cp.start()

    quarter = WHOLE + x * QUARTER

    def wz(i):
        piece = wsame.at[z, c]
        return rcopy(piece, piece, WZ + i, dev_z(1 if i == 0 else 3))

    def wf(i):
        piece = wsame.at[(z + (3 if i == 0 else 1)) % 4, c, pl.ds(i * 160, 160)]
        return rcopy(piece, piece, WF + i, dev_z(1 if i == 0 else 3))

    def wy(dz, way, part):
        zz = (z + dz) % 4
        first = (way * (WHOLE // 2), pl.multiple_of(quarter + way * (QUARTER // 2), 16))[part]
        rows = pl.ds(first, (WHOLE // 2, QUARTER // 2)[part])
        return rcopy(
            wsame.at[zz, c, rows],
            wother.at[zz, c, rows],
            WY + (dz * 2 + way) * 2 + part,
            dev_y(1 if way == 0 else 3),
        )

    def wx(dz, d):
        piece = wother.at[(z + dz) % 4, c, pl.ds(pl.multiple_of(quarter, 32), QUARTER)]
        return rcopy(piece, piece, WX + dz * 3 + d - 1, dev_x(d))

    def wy_start(dz):
        for way in range(2):
            for part in range(2):
                wy(dz, way, part).start()

    def spread(dz):
        for way in range(2):
            for part in range(2):
                wy(dz, way, part).wait()
        for d in (2, 1, 3):
            wx(dz, d).start()

    def arrived(dz):
        for d in (1, 2, 3):
            wx(dz, d).wait()
        ws(dz, 1).start()

    def ws(dz, other):
        piece = (wother if other else wsame).at[(z + dz) % 4, c]
        return rcopy(piece, piece, WS + other * 4 + dz, sib)

    def part_out(dz):
        zz = (z + dz) % 4
        cols = pl.ds(pl.multiple_of(zz * 640, 640), 640)
        return pltpu.make_async_copy(x_own.at[:, cols], part_hbm.at[zz], lsem.at[11 + dz])

    def input_grad(dz):
        ws(dz, 0).wait()

        @pl.loop(0, 2)
        def _(half):
            zz = (z + dz) % 4
            cols = pl.ds(pl.multiple_of(zz * 640, 640), 640)
            rows = pl.ds(pl.multiple_of(half * 256, 256), 256)
            x_own[rows, cols] = lax.dot_general(
                u[rows], wsame[zz].reshape(640, 1024), NT, preferred_element_type=f32
            ).astype(bf16)

        part_out(dz).start()

    for i in range(2):
        wz(i).start()
    wy_start(0)

    def hidden_copy(j):
        to = (f + j) % 16
        cols = pl.ds(pl.multiple_of((to // 2) * 640, 640), 640)
        return rcopy(hidden.at[:, cols], hr.at[j], HS + j, (to, t))

    @pl.loop(1, 16)
    def _(j):
        hidden_copy(j).start()

    hr[0] = hidden[:, pl.ds(pl.multiple_of((f // 2) * 640, 640), 640)]
    wpad[...] = jnp.zeros_like(wpad)

    right, left = (x + 1) % 4, (x + 3) % 4

    def two_hop(i, zz, k):
        return rcopy(
            ga.at[(x + 2) % 4, i, zz], t1.at[i, zz], T1 + i * 4 + k, dev_x(1 if i == 0 else 3)
        )

    def direct(i, zz, k):
        piece = ga.at[right if i == 0 else left, 1 - i, zz]
        return rcopy(piece, r1a.at[i, 1 - i, zz], D1 + i * 4 + k, dev_x(1 if i == 0 else 3))

    def summed(i, zz, k):
        piece = ga.at[right if i == 0 else left, i, zz]
        return rcopy(piece, r1a.at[i, i, zz], F1 + i * 4 + k, dev_x(1 if i == 0 else 3))

    def b1(d, zz, k):
        yy = (y + d) % 4
        return rcopy(
            gb.at[:, yy // 2, zz, yy % 2], r1b.at[d - 1, :, zz], B1 + (d - 1) * 4 + k, dev_y(d)
        )

    def b2(d):
        return rcopy(s1b.at[:, (z + d) % 4], r2b.at[d - 1], B2 + d - 1, dev_z(d))

    def b3(d):
        return rcopy(s2b.at[(x + d) % 4], r3b.at[d - 1], B3 + d - 1, dev_x(d))

    def c1(d):
        return rcopy(gc.at[:, :, (z + d) % 4], r1c.at[d - 1], C1 + d - 1, dev_z(d))

    def a2(d, zz, k):
        yy = (y + d) % 4
        return rcopy(
            s1a.at[yy // 2, zz, yy % 2], r2a.at[d - 1, zz], A2 + (d - 1) * 4 + k, dev_y(d)
        )

    def c2(d):
        return rcopy(s1c.at[(x + d) % 4], r2c.at[d - 1], C2 + d - 1, dev_x(d))

    def a3(d):
        return rcopy(s2a.at[(z + d) % 4], r3a.at[d - 1], A3 + d - 1, dev_z(d))

    def c3(d):
        yy = (y + d) % 4
        return rcopy(s2c.at[yy // 2, yy % 2], r3c.at[d - 1], C3 + d - 1, dev_y(d))

    def pass_on(k):
        zz = (z + 1 + k) % 4
        for i in range(2):
            two_hop(i, zz, k).wait()
            to = right if i == 0 else left

            @pl.loop(0, 2)
            def _(ll):
                got = ga[to, i, zz, ll].astype(f32) + t1[i, zz, ll].astype(f32)
                ga[to, i, zz, ll] = got.astype(bf16)

            summed(i, zz, k).start()

    ut_copy.wait()
    for k in range(4):
        zz = (z + 1 + k) % 4
        local[1 + k].wait()
        sib_copies[k].wait()
        if k < 2:
            sib_copies[k + 2].start()

        @pl.loop(0, 4)
        def _(i):
            ll, half = i // 2, i % 2
            cols = pl.ds(pl.multiple_of(zz * 1280 + ll * 640, 640), 640)
            rows = pl.ds(pl.multiple_of(half * 256, 256), 256)
            part = jnp.dot(ut[c, rows], x_own[:, cols], preferred_element_type=f32)
            part += jnp.dot(ut_sib[rows], x_sib[:, cols], preferred_element_type=f32)
            part = part.astype(bf16)
            for b in range(4):
                xx, hh = half * 2 + b // 2, b % 2
                ga[xx, hh, zz, ll] = part[b * 64 : (b + 1) * 64, 0:384]
                gb[xx, hh, zz, ll] = part[b * 64 : (b + 1) * 64, 384:512]
                gc[xx, hh, zz, ll] = part[b * 64 : (b + 1) * 64, 512:640]

        for i in range(2):
            two_hop(i, zz, k).start()
        for i in range(2):
            direct(i, zz, k).start()
        for d in (2, 1, 3):
            b1(d, zz, k).start()
        if k < 3:
            c1(k + 1).start()
        if k > 0:
            pass_on(k - 1)
        if k == 1:
            for cp in local[5:]:
                cp.start()
            ws(0, 0).start()

    for i in range(2):
        wz(i).wait()
    for i in range(2):
        wf(i).start()
    for dz in (1, 3):
        wy_start(dz)
        ws(dz, 0).start()
    pass_on(3)


    local[5].wait()
    fresh_out[0] = jnp.dot(hidden[...], kw[...], preferred_element_type=f32).astype(bf16)
    qf[...] = jnp.zeros_like(qf)
    for step in range(4):
        for g in range(GROUP):
            qf[:, step * GROUP + g] = queries[step, :, g * HD : (g + 1) * HD].astype(f32)
    local[6].wait()
    local[7].wait()
    scale = 1.0 / math.sqrt(HD)

    def attend(r):
        q = qf[r].astype(bf16)
        scores = lax.dot_general(q, keys[r], NT, preferred_element_type=f32) * scale
        slots = lax.broadcasted_iota(jnp.int32, (32, 4096), 1)
        scores = jnp.where(slots < lengths[r], scores, -1e30)
        extra = lax.dot_general(q, fresh_out[0], NT, preferred_element_type=f32) * scale
        line = lax.broadcasted_iota(jnp.int32, (32, 16), 0)
        item = lax.broadcasted_iota(jnp.int32, (32, 16), 1)
        seen = ((item & 3) == r) & ((item >> 2) * GROUP <= line)
        extra = jnp.where(seen, extra, -1e30)
        highest = jnp.maximum(
            jnp.max(scores, axis=1, keepdims=True), jnp.max(extra, axis=1, keepdims=True)
        )
        scores = jnp.exp(scores - highest)
        extra = jnp.exp(extra - highest)
        norm = 1.0 / (
            jnp.sum(scores, axis=1, keepdims=True) + jnp.sum(extra, axis=1, keepdims=True)
        )
        fprob[r] = (extra * norm).astype(bf16)
        acc[r] = jnp.dot((scores * norm).astype(bf16), values[r], preferred_element_type=f32)

    def total(own, others, index, count=3):
        got = own.astype(f32)
        for d in range(count):
            got += others[(d,) + index].astype(f32)
        return got

    def first(k):
        zz = (z + 1 + k) % 4
        for i in range(2):
            direct(i, zz, k).wait()
            summed(i, zz, k).wait()

        @pl.loop(0, 4)
        def _(i):
            hh, ll = i // 2, i % 2
            s1a[hh, zz, ll] = total(ga[x, hh, zz, ll], r1a, (hh, zz, ll), 2).astype(bf16)

        for d in (2, 1, 3):
            a2(d, zz, k).start()

    def second(k):
        zz = (z + 1 + k) % 4
        for d in (1, 2, 3):
            a2(d, zz, k).wait()
        s2a[zz] = total(s1a[yh, zz, yl], r2a, (zz,))
        if k < 3:
            a3(k + 1).start()

    def first_b(k):
        zz = (z + 1 + k) % 4
        for d in (1, 2, 3):
            b1(d, zz, k).wait()

        @pl.loop(0, 4)
        def _(i):
            s1b[i, zz] = total(gb[i, yh, zz, yl], r1b, (i, zz)).astype(bf16)

        if k < 3:
            b2(k + 1).start()

    def second_b():
        for d in (1, 2, 3):
            b2(d).wait()

        @pl.loop(0, 4)
        def _(i):
            s2b[i] = total(s1b[i, z], r2b, (i,))

        for d in (2, 1, 3):
            b3(d).start()

    def first_c():
        for d in (1, 2, 3):
            c1(d).wait()

        @pl.loop(0, 16)
        def _(i):
            xx, hh, ll = i // 4, (i // 2) % 2, i % 2
            s1c[xx, hh, ll] = total(gc[xx, hh, z, ll], r1c, (xx, hh, ll)).astype(bf16)

        for d in (2, 1, 3):
            c2(d).start()

    def second_c():
        for d in (1, 2, 3):
            c2(d).wait()

        @pl.loop(0, 4)
        def _(i):
            hh, ll = i // 2, i % 2
            s2c[hh, ll] = total(s1c[x, hh, ll], r2c, (hh, ll))

        for d in (2, 1, 3):
            c3(d).start()

    first(0)
    first_b(0)
    pl.loop(0, 1)(attend)
    first(1)
    first_b(1)
    pl.loop(1, 2)(attend)
    spread(0)
    input_grad(0)
    first(2)
    first_b(2)
    for i in range(2):
        wf(i).wait()
    wy_start(2)
    ws(2, 0).start()
    first_c()
    second(0)
    pl.loop(2, 3)(attend)
    pl.loop(3, 4)(attend)
    first(3)
    first_b(3)
    input_grad(1)
    second(1)
    second_c()
    second_b()
    spread(1)
    spread(3)
    second(2)
    second(3)
    spread(2)
    input_grad(3)

    for d in (1, 2, 3):
        a3(d).wait()
        b3(d).wait()
        c3(d).wait()
    gx[c, :, 0:384] = total(s2a[z], r3a, ()) * grad_factor
    gx[c, :, 384:512] = total(s2b[x], r3b, ()) * grad_factor
    gx[c, :, 512:640] = total(s2c[yh, yl], r3c, ()) * grad_factor
    gx_copy = rcopy(gx.at[c], gx.at[c], GX, sib)
    gx_copy.start()
    gx_copy.wait()
    gt[...] = gx[...].reshape(128, 640).T
    mine = pl.ds(pl.multiple_of(c * 320, 320), 320)
    gown[...] = gt[mine, :].astype(bf16)
    grad_out.start()

    def tp_copy(j):
        return rcopy(gown, gall.at[t], TP + j, (f, (t + j) % 8))

    @pl.loop(1, 8)
    def _(j):
        tp_copy(j).start()

    local[8].wait()
    local[9].wait()
    stepped, _ = adamw(master[:, tcols], gown[...].astype(f32), m1[...], m2[...])
    wpad[mine, :] = stepped.astype(bf16)

    @pl.loop(1, 16)
    def _(j):
        hidden_copy(j).wait()

    pf[...] = jnp.dot(
        hr[...].reshape(256, 640), wpad[...], preferred_element_type=f32
    ).reshape(16, 16, 128)

    def fresh_copy(j):
        return rcopy(pf.at[j], fr.at[j], FR + j, ((f + 16 - j) % 16, t))

    @pl.loop(1, 16)
    def _(j):
        fresh_copy(j).start()

    for dz in (0, 1, 3, 2):
        arrived(dz)
    input_grad(2)

    @pl.loop(1, 16)
    def _(j):
        fresh_copy(j).wait()

    fr[0] = pf[0]
    fresh_out[1] = jnp.sum(fr[...], axis=0).astype(bf16)

    @pl.loop(0, 4)
    def _(r):
        acc[r] += jnp.dot(fprob[r], fresh_out[1], preferred_element_type=f32)

    for step in range(4):
        for g in range(GROUP):
            attended[step, :, g * HD : (g + 1) * HD] = acc[:, step * GROUP + g].astype(bf16)

    grad_out.wait()

    @pl.loop(1, 8)
    def _(j):
        tp_copy(j).wait()

    for dz in range(4):
        ws(dz, 1).wait()
        part_out(dz).wait()


def learn(
    inputs, upstream, master, m1, m2, flat, key_weight, queries, keys, values, lengths, grad_factor
):
    hbm = pl.BlockSpec(memory_space=pl.ANY)
    vmem = pl.BlockSpec(memory_space=pltpu.VMEM)
    smem = pl.BlockSpec(memory_space=pltpu.SMEM)
    shape = jax.ShapeDtypeStruct
    V = pltpu.VMEM
    scratch = [
        V((16, 5120), f32),
        V((16, 5120), bf16),
        V((2, 512, 512), bf16),
        V((4, 2, 320, 1024), bf16),
        V((5120, 128), bf16),
        V((4, 4096, 128), bf16),
        V((4, 4096, 128), bf16),
        V((4, 32, 128), f32),
        V((4, 32, 128), f32),
        V((4, 32, 16), bf16),
        V((512, 5120), bf16),
        V((512, 5120), bf16),
        V((512, 512), bf16),
        V((320, 1024), f32),
        V((320, 128), f32),
        V((320, 128), f32),
        V((4, 2, 4, 2, 64, 384), bf16),
        V((4, 2, 4, 2, 64, 128), bf16),
        V((4, 2, 4, 2, 64, 128), bf16),
        V((2, 4, 2, 64, 384), bf16),
        V((2, 2, 4, 2, 64, 384), bf16),
        V((3, 4, 4, 64, 128), bf16),
        V((3, 4, 2, 2, 64, 128), bf16),
        V((2, 4, 2, 64, 384), bf16),
        V((4, 4, 64, 128), bf16),
        V((4, 2, 2, 64, 128), bf16),
        V((3, 4, 64, 384), bf16),
        V((3, 4, 64, 128), bf16),
        V((3, 2, 2, 64, 128), bf16),
        V((4, 64, 384), f32),
        V((4, 64, 128), f32),
        V((2, 2, 64, 128), f32),
        V((3, 64, 384), f32),
        V((3, 64, 128), f32),
        V((3, 64, 128), f32),
        V((2, 64, 640), f32),
        V((640, 128), f32),
        V((320, 128), bf16),
        V((640, 128), bf16),
        V((16, 16, 640), bf16),
        V((16, 16, 128), f32),
        V((16, 16, 128), f32),
        pltpu.SemaphoreType.DMA((SEMS,)),
        pltpu.SemaphoreType.DMA((SEMS,)),
        pltpu.SemaphoreType.DMA((15,)),
    ]
    return pl.pallas_call(
        functools.partial(learn_kernel, grad_factor),
        out_shape=(
            shape((4, 2, 320, 1024), bf16),
            shape((8, 320, 128), bf16),
            shape((4, 512, 640), bf16),
            shape((2, 16, 128), bf16),
            shape((4, 4, 640), bf16),
        ),
        in_specs=[hbm, vmem, hbm, hbm, hbm, vmem, hbm, vmem, hbm, hbm, smem],
        out_specs=[hbm, hbm, hbm, vmem, vmem],
        scratch_shapes=scratch,
        name="learn",
        compiler_params=pltpu.CompilerParams(
            collective_id=0, has_side_effects=True, vmem_limit_bytes=56 << 20
        ),
    )(inputs, upstream, master, m1, m2, flat, key_weight, queries, keys, values, lengths)


def finish_kernel(
    u, part, w, grad, master, m1, m2, fresh, heads, input_grad, new_master, new_moment, kv, attended
):
    @pl.when(pl.program_id(0) == 0)
    def _():
        wide = fresh[...].astype(f32).reshape(2, 4, 4, 128)
        kv[...] = jnp.stack([wide[0], wide[1]], axis=2).astype(bf16)
        attended[...] = heads[...]

    yl = (lax.axis_index("fsdp") // 2) % 2
    same = pl.ds(pl.multiple_of(yl * 640, 640), 640)
    other = pl.ds(pl.multiple_of((1 - yl) * 640, 640), 640)
    input_grad[:, same] = part[...]
    input_grad[:, other] = lax.dot_general(
        u[...], w[...], NT, preferred_element_type=f32
    ).astype(bf16)
    for i in range(2):
        cols = slice(i * 128, (i + 1) * 128)
        new_master[:, cols], new_moment[:, cols] = adamw(
            master[:, cols], grad[i].astype(f32), m1[:, cols], m2[:, cols]
        )


def finish(upstream, part, weight, grad, master, m1, m2, fresh, heads):
    vmem = pl.BlockSpec(memory_space=pltpu.VMEM)
    cols = pl.BlockSpec((320, 256), lambda i: (0, i))
    return pl.pallas_call(
        finish_kernel,
        grid=(4,),
        out_shape=(
            jax.ShapeDtypeStruct((512, 5120), bf16),
            jax.ShapeDtypeStruct((320, 1024), f32),
            jax.ShapeDtypeStruct((320, 1024), f32),
            jax.ShapeDtypeStruct((4, 4, 2, 128), bf16),
            jax.ShapeDtypeStruct((4, 4, 640), bf16),
        ),
        in_specs=[
            pl.BlockSpec((512, 1024), lambda i: (0, 0)),
            pl.BlockSpec((None, 512, 640), lambda i: (i, 0, 0)),
            pl.BlockSpec((640, 1024), lambda i: (i, 0)),
            pl.BlockSpec((2, 320, 128), lambda i: (i, 0, 0)),
            cols,
            cols,
            cols,
            vmem,
            vmem,
        ],
        out_specs=[pl.BlockSpec((512, 1280), lambda i: (0, i)), cols, cols, vmem, vmem],
        name="finish",
        compiler_params=pltpu.CompilerParams(vmem_limit_bytes=60 << 20),
    )(upstream, part, weight, grad, master, m1, m2, fresh, heads)


def shards(
    inputs,
    upstream,
    master,
    moment_one,
    moment_two,
    hidden_steps,
    key_weight,
    queries,
    key_cache,
    value_cache,
    lengths,
):
    grad_factor = 1.0 / math.sqrt(inputs.shape[0] * lax.axis_size("fsdp") * lax.axis_size("tp"))
    weight, grad, part, fresh, attended = learn(
        inputs,
        upstream,
        master,
        moment_one,
        moment_two,
        hidden_steps,
        key_weight,
        queries,
        key_cache,
        value_cache,
        lengths,
        grad_factor,
    )
    return finish(
        upstream,
        part,
        weight.reshape(2560, 1024),
        grad,
        master,
        moment_one,
        moment_two,
        fresh,
        attended,
    )


def solution(mesh):
    in_specs = (
        P(("fsdp", "tp"), None),
        P(("fsdp", "tp"), None),
        P("fsdp", None),
        P("fsdp", None),
        P("fsdp", None),
        P(None, "fsdp", None),
        P(None, "tp"),
        P(None, "fsdp", "tp"),
        P("fsdp", None, "tp"),
        P("fsdp", None, "tp"),
        P("fsdp"),
    )
    out_specs = (
        P(("fsdp", "tp"), None),
        P("fsdp", None),
        P("fsdp", None),
        P(None, "fsdp", None, "tp"),
        P(None, "fsdp", "tp"),
    )
    return jax.shard_map(shards, mesh=mesh, in_specs=in_specs, out_specs=out_specs, check_vma=False)
```
